32 devices in a mesh: depth: 4 (over z), rows: 8 (over y, x, core).
Axes of the slice: x: 2, y: 2, z: 4, core: 2. Of those that a mesh axis runs over, the one named last changes fastest.
Arguments:
- node_feat: bfloat16 [512, 8192], P('depth', 'rows'), may hold values from -6 to 6
- grad_out: bfloat16 [512, 8192], P('depth', 'rows'), may hold values from -0.25 to 0.25
- adjacency: bfloat16 [128, 256, 256], P('rows'), may hold values from -0.1875 to 0.1875
- tile_count: int32 [8], replicated, may hold values from 4 to 16, as said below
- tile_row: int32 [8, 16], replicated, may hold values from 0 to 3, as said below
- tile_col: int32 [8, 16], replicated, may hold values from 0 to 31, as said below
Outputs:
- weight_grad: float32 [8, 16, 256, 256], P('rows', 'depth')
The draws below stay inside these ranges and needn't reach their ends.
Inputs may be any that keep to these rules, and one draw needn't show every extreme that they name: `tile_count`: the number of live slots of each owner; one owner has exactly 16 in every draw. `tile_row`: 0 in dead slots. `tile_col`: 0 in dead slots. An owner's live slots name distinct column tiles; at most 2 of them lie among the node tiles of any one owner (column tile // 4), and every owner has exactly 2 from some owner.
All inputs are finite; a program needn't handle non-finite values.
Results may differ from the reference program's by a relative error of at most 0.0029.
Values may be sent and summed in bfloat16 or wider, within the bound.
A program may use at most 64 MiB of HBM per device.

```python
import jax
import jax.numpy as jnp
from jax import lax

TILE = 256
FEAT = 512
TROWS_DEV = 4
PAIR_MOST = 2
SLOTS = 16
NTILES = 32
NODES = 8192
N_DEPTH = 4
N_ROWS = 8


def tile_layout(key):
    counts = jax.random.randint(jax.random.fold_in(key, 11), (N_ROWS,), SLOTS // 4, 3 * SLOTS // 4 + 1)
    busiest = jax.random.randint(jax.random.fold_in(key, 12), (), 0, N_ROWS)
    owner_ids = jnp.arange(N_ROWS, dtype=jnp.int32)
    counts = jnp.where(owner_ids == busiest, SLOTS, counts).astype(jnp.int32)
    scores = jax.random.randint(jax.random.fold_in(key, 13), (N_ROWS, N_ROWS), 1, 1 << 16) * N_ROWS
    scores = scores + owner_ids[None, :]
    forced = (owner_ids[:, None] == busiest) & (owner_ids[None, :] == N_ROWS - 1)
    scores = jnp.where(forced, 0, scores)
    owner_order = jnp.argsort(scores, axis=1).astype(jnp.int32)
    slot_ids = jnp.arange(SLOTS, dtype=jnp.int32)
    leading = slot_ids < PAIR_MOST
    remaining = jnp.maximum(slot_ids - PAIR_MOST, 0)
    rank_of = jnp.where(leading, slot_ids, remaining // (N_ROWS - 1))
    pick_index = jnp.where(leading, 0, 1 + remaining % (N_ROWS - 1))
    owners = jnp.take_along_axis(owner_order, jnp.broadcast_to(pick_index[None, :], (N_ROWS, SLOTS)), axis=1)
    offsets = jax.random.randint(jax.random.fold_in(key, 14), (N_ROWS, N_ROWS), 0, TROWS_DEV)
    offsets = jnp.where(forced, TROWS_DEV - 1, offsets)
    offsets_here = jnp.take_along_axis(offsets, owners, axis=1)
    columns = owners * TROWS_DEV + (offsets_here + rank_of[None, :]) % TROWS_DEV
    row_ids = jax.random.randint(jax.random.fold_in(key, 15), (N_ROWS, SLOTS), 0, TROWS_DEV)
    first_busy = (owner_ids[:, None] == busiest) & (slot_ids[None, :] == 0)
    row_ids = jnp.where(first_busy, TROWS_DEV - 1, row_ids)
    is_live = slot_ids[None, :] < counts[:, None]
    columns = jnp.where(is_live, columns, 0).astype(jnp.int32)
    row_ids = jnp.where(is_live, row_ids, 0).astype(jnp.int32)
    return (counts, row_ids, columns)


def draw_tile_count(key, part):
    return tile_layout(key)[0]


def draw_tile_row(key, part):
    return tile_layout(key)[1]


def draw_tile_col(key, part):
    return tile_layout(key)[2]


def block_scale(stream_key, shape, cuts, smallest, top_value):
    level = 1.0
    for position, shards_of in cuts:
        steps = jax.random.uniform(jax.random.fold_in(jax.random.fold_in(stream_key, 6), position), (shards_of,), jnp.float32, smallest / len(cuts), top_value / len(cuts))
        level = level * jnp.repeat(jnp.exp(steps), shape[position] // shards_of).reshape((-1,) + (1,) * (len(shape) - 1 - position))
    return level


def gaussian(rng, extent, width, most, shards=(), held_as=jnp.bfloat16):
    drawn = jax.random.normal(rng, extent, jnp.float32) * width
    if len(shards) > 0:
        drawn = block_scale(rng, extent, shards, -0.22, 0.18) * drawn
    return jnp.clip(drawn, min=-most, max=most).astype(held_as)


def setup_inputs(seed: int = 0) -> dict:
    streams_of = jax.random.split(jax.random.key(seed), 7)
    node_feat = gaussian(streams_of[0], (FEAT, NODES), 1.0, 6.0, ((0, 4), (1, 8)))
    grad_out = gaussian(streams_of[1], (FEAT, NODES), FEAT ** -0.5, 0.25, ((0, 4), (1, 8)))
    adjacency = gaussian(streams_of[2], (N_ROWS * SLOTS, TILE, TILE), (4 * TILE) ** -0.5, 0.1875, ((0, 8),))
    tile_count = draw_tile_count(jax.random.fold_in(streams_of[6], 71), 0)
    tile_row = draw_tile_row(jax.random.fold_in(streams_of[6], 71), 0)
    tile_col = draw_tile_col(jax.random.fold_in(streams_of[6], 71), 0)
    return dict(node_feat=node_feat, grad_out=grad_out, adjacency=adjacency, tile_count=tile_count, tile_row=tile_row, tile_col=tile_col)


top_precision = lax.Precision.HIGHEST


def reference(node_feat, grad_out, adjacency, tile_count, tile_row, tile_col):
    feat_tiles = node_feat.astype(jnp.float32).reshape(FEAT, NTILES, TILE)
    grad_tiles = grad_out.astype(jnp.float32).reshape(FEAT, NTILES, TILE)
    owner_tiles = adjacency.astype(jnp.float32).reshape(N_ROWS, SLOTS, TILE, TILE)
    slot_ids = jnp.arange(SLOTS, dtype=jnp.int32)
    is_live = (slot_ids[None, :] < tile_count[:, None]).astype(jnp.float32)
    global_rows = (jnp.arange(N_ROWS, dtype=jnp.int32)[:, None] * TROWS_DEV + tile_row).astype(jnp.int32)
    global_cols = tile_col.astype(jnp.int32)

    def accumulate(running, inputs):
        summed_h, summed_g = running
        tiles_here, rows_here, cols_here, live_here = inputs
        weights = tiles_here * live_here[:, None, None]
        h_terms = jnp.einsum("fsb,sab->fsa", feat_tiles[:, cols_here], weights, precision=top_precision)
        g_terms = jnp.einsum("fsa,sab->fsb", grad_tiles[:, rows_here], weights, precision=top_precision)
        return (summed_h.at[:, rows_here].add(h_terms), summed_g.at[:, cols_here].add(g_terms)), None

    zero_field = jnp.zeros((FEAT, NTILES, TILE), jnp.float32)
    totals, unused = lax.scan(accumulate, (zero_field, zero_field), (owner_tiles, global_rows, global_cols, is_live))
    h_round = lax.optimization_barrier(totals[0].astype(jnp.bfloat16)).astype(jnp.float32)
    g_round = lax.optimization_barrier(totals[1].astype(jnp.bfloat16)).astype(jnp.float32)
    group_size = FEAT // N_DEPTH

    def tile_grads(inputs):
        rows_here, cols_here, live_here = inputs
        dy_rows = grad_tiles[:, rows_here].reshape(N_DEPTH, group_size, SLOTS, TILE)
        g_rows = g_round[:, rows_here].reshape(N_DEPTH, group_size, SLOTS, TILE)
        h_cols = h_round[:, cols_here].reshape(N_DEPTH, group_size, SLOTS, TILE)
        x_cols = feat_tiles[:, cols_here].reshape(N_DEPTH, group_size, SLOTS, TILE)
        parts = jnp.einsum("qfsa,qfsb->qsab", dy_rows, h_cols, precision=top_precision)
        parts = parts + jnp.einsum("qfsa,qfsb->qsab", g_rows, x_cols, precision=top_precision)
        return jnp.sum(parts, axis=0) * live_here[:, None, None]

    return lax.map(tile_grads, (global_rows, global_cols, is_live))
```

```python
import functools

import jax
import jax.numpy as jnp
from jax import lax
from jax.experimental import pallas as pl
from jax.experimental.pallas import tpu as pltpu
from jax.sharding import PartitionSpec as P

MESH = pl.DeviceIdType.MESH
F32 = jnp.float32
BF16 = jnp.bfloat16


def flip(index, mask):
    bit = 1
    out = index
    while bit <= mask:
        if mask & bit:
            out = out + bit * (1 - 2 * ((index // bit) % 2))
        bit *= 2
    return out


def bit_orders(rows):
    bits = []
    bit = 1
    while bit < rows:
        bits.append(bit)
        bit *= 2
    core, chip = bits[:1], bits[1:]
    half = len(chip) // 2
    x_bits, y_bits = chip[:half], chip[half:]
    return (y_bits + x_bits + core, x_bits + y_bits + core)


class Gather:
    def __init__(self, rows, tiles, buf, send_sem, recv_sem, depth_id, me):
        self.rows, self.tiles, self.buf = rows, tiles, buf
        self.send_sem, self.recv_sem = send_sem, recv_sem
        self.depth_id, self.me = depth_id, me
        self.orders = bit_orders(rows)

    def mask(self, half, place):
        out = 0
        for n, bit in enumerate(self.orders[half]):
            if place >> n & 1:
                out |= bit
        return out

    def copy(self, half, place, n):
        mask = self.mask(half, place)
        bit = self.orders[half][n]
        part = self.tiles // 2
        block = flip(self.me, mask)
        ref = self.buf.at[pl.ds(block * self.tiles + half * part, part)]
        sem = half * self.rows + (mask | bit)
        return pltpu.make_async_remote_copy(
            src_ref=ref,
            dst_ref=ref,
            send_sem=self.send_sem.at[sem],
            recv_sem=self.recv_sem.at[sem],
            device_id=(self.depth_id, flip(self.me, bit)),
            device_id_type=MESH,
        )

    def incoming(self, half, place):
        mask = self.mask(half, place)
        part = self.tiles // 2
        ref = self.buf.at[pl.ds(flip(self.me, mask) * self.tiles + half * part, part)]
        sem = half * self.rows + mask
        return pltpu.make_async_remote_copy(
            src_ref=ref,
            dst_ref=ref,
            send_sem=self.send_sem.at[sem],
            recv_sem=self.recv_sem.at[sem],
            device_id=(self.depth_id, flip(self.me, mask)),
            device_id_type=MESH,
        )

    def start(self):
        for n in range(len(self.orders[0])):
            for half in range(2):
                self.copy(half, 0, n).start()

    def forward(self, begin, end):
        count = len(self.orders[0])
        for place in range(begin, end):
            for half in range(2):
                self.incoming(half, place).wait_recv()
                for n in range(place.bit_length(), count):
                    self.copy(half, place, n).start()

    def drain(self):
        count = len(self.orders[0])
        for place in range(self.rows // 2):
            for half in range(2):
                for n in range(place.bit_length(), count):
                    self.copy(half, place, n).wait_send()


def kernel(
    rows,
    depth,
    x_hbm,
    dy_hbm,
    adj_hbm,
    cnt,
    trow,
    tcol,
    out,
    xbuf,
    hbuf,
    adj,
    dyt,
    dy_t,
    g_t,
    terms,
    gout,
    gin,
    gacc,
    send_up,
    send_dn,
    recv_up,
    recv_dn,
    local_sem,
    xs_sem,
    xr_sem,
    hs_sem,
    hr_sem,
    gs_sem,
    gr_sem,
    us_sem,
    ur_sem,
    ds_sem,
    dr_sem,
):
    d = lax.axis_index("depth")
    me = lax.axis_index("rows")
    feat = xbuf.shape[1]
    tile = xbuf.shape[2]
    tiles = dyt.shape[0]
    slots = adj.shape[0]
    share = slots // depth

    local = []
    for j in range(tiles):
        cols = pl.ds(j * tile, tile)
        local.append(
            pltpu.make_async_copy(x_hbm.at[:, cols], xbuf.at[me * tiles + j], local_sem.at[j])
        )
    for j in range(tiles):
        cols = pl.ds(j * tile, tile)
        local.append(
            pltpu.make_async_copy(dy_hbm.at[:, cols], dyt.at[j], local_sem.at[tiles + j])
        )
    local.append(pltpu.make_async_copy(adj_hbm, adj, local_sem.at[2 * tiles]))
    for c in local:
        c.start()

    barrier = pltpu.get_barrier_semaphore()
    for t in range(1, rows):
        pl.semaphore_signal(
            barrier, inc=1, device_id=(d, (me + t) % rows), device_id_type=MESH
        )

    for t in range(1, depth):
        pl.semaphore_signal(
            barrier, inc=1, device_id=((d + t) % depth, me), device_id_type=MESH
        )
    pl.semaphore_wait(barrier, rows - 1 + depth - 1)

    for c in local[:tiles]:
        c.wait()
    xg = Gather(rows, tiles, xbuf, xs_sem, xr_sem, d, me)
    hg = Gather(rows, tiles, hbuf, hs_sem, hr_sem, d, me)
    xg.start()
    for c in local[tiles:]:
        c.wait()

    my_count = cnt[me]

    def g_term(slot, valid):
        row = trow[me, slot]
        g = jnp.dot(dyt[row], adj[slot], preferred_element_type=F32)
        return jnp.where(valid, g, 0.0).astype(BF16)

    def g_body(t, carry):
        o = (me + t) % rows
        first = jnp.int32(0)
        last = jnp.int32(0)
        seen = jnp.int32(0)
        for s in range(slots):
            hit = (s < my_count) & (lax.div(tcol[me, s], jnp.int32(tiles)) == o)
            last = jnp.where(hit, s, last)
            first = jnp.where(hit & (seen == 0), s, first)
            seen = jnp.where(hit, 1, seen)
        gout[t, 0] = g_term(first, seen > 0)
        gout[t, 1] = g_term(last, last > first)
        return carry

    lax.fori_loop(0, rows, g_body, 0)

    for j in range(tiles):
        dy_t[j] = dyt[j].astype(F32).T.astype(BF16)

    def g_copy(t):
        return pltpu.make_async_remote_copy(
            src_ref=gout.at[t],
            dst_ref=gin.at[t],
            send_sem=gs_sem.at[t],
            recv_sem=gr_sem.at[t],
            device_id=(d, (me + t) % rows),
            device_id_type=MESH,
        )

    xg.forward(1, rows // 2)
    for t in range(1, rows):
        g_copy(t).start()
    gin[0] = gout[0]
    xg.forward(rows // 2, rows)

    def h_body(s, carry):
        h = lax.dot_general(
            xbuf[tcol[me, s]], adj[s], (((1,), (1,)), ((), ())), preferred_element_type=F32
        )
        terms[s] = jnp.where(s < my_count, h, 0.0)
        return carry

    lax.fori_loop(0, slots, h_body, 0)

    chunk = min(32, feat)

    def h_sum(c, carry):
        at = pl.ds(pl.multiple_of(c * chunk, chunk), chunk)
        total = [jnp.zeros((chunk, tile), F32) for _ in range(tiles)]
        for s in range(slots):
            term = terms[s, at, :]
            row = trow[me, s]
            for i in range(tiles):
                total[i] = total[i] + jnp.where(row == i, term, 0.0)
        for i in range(tiles):
            hbuf[me * tiles + i, at, :] = total[i].astype(BF16)
        return carry

    lax.fori_loop(0, feat // chunk, h_sum, 0)
    hg.start()

    for t in range(1, rows):
        g_copy(t).wait_recv()
    gacc[...] = jnp.zeros_like(gacc)

    def g_sum(t, carry):
        p = (me + rows - t) % rows
        count = cnt[p]
        seen = jnp.int32(0)
        rank = [jnp.int32(0) for _ in range(tiles)]
        flag = [jnp.int32(0) for _ in range(tiles)]
        for s in range(slots):
            col = tcol[p, s]
            live = s < count
            for j in range(tiles):
                hit = live & (col == me * tiles + j)
                rank[j] = jnp.where(hit, seen, rank[j])
                flag[j] = jnp.where(hit, 1, flag[j])
            seen = jnp.where(live & (lax.div(col, jnp.int32(tiles)) == me), 1, seen)
        for j in range(tiles):
            term = gin[t, rank[j]].astype(F32)
            gacc[j] += jnp.where(flag[j] > 0, term, 0.0)
        return carry

    lax.fori_loop(0, rows, g_sum, 0)
    for j in range(tiles):
        g_t[j] = gacc[j].astype(BF16).astype(F32).T.astype(BF16)

    hg.forward(1, rows)

    def partial(s):
        row = trow[me, s]
        col = tcol[me, s]
        p = jnp.dot(dy_t[row], hbuf[col], preferred_element_type=F32)
        p = p + jnp.dot(g_t[row], xbuf[col], preferred_element_type=F32)
        return jnp.where(s < my_count, p, 0.0)

    def up_copy(s):
        return pltpu.make_async_remote_copy(
            src_ref=send_up.at[s],
            dst_ref=recv_up.at[s],
            send_sem=us_sem.at[s],
            recv_sem=ur_sem.at[s],
            device_id=(lax.rem(d + 1, depth), me),
            device_id_type=MESH,
        )

    def dn_copy(s):
        return pltpu.make_async_remote_copy(
            src_ref=send_dn.at[s],
            dst_ref=recv_dn.at[s],
            send_sem=ds_sem.at[s],
            recv_sem=dr_sem.at[s],
            device_id=(lax.rem(d + depth - 1, depth), me),
            device_id_type=MESH,
        )

    def z_body(n, carry):
        i = n // share
        k = n % share
        t_up = depth - 1 - i
        s_up = t_up * share + k

        @pl.when(t_up > d)
        def _():
            send_up[s_up] = partial(s_up).astype(BF16)

            @pl.when(d > 0)
            def _():
                up_copy(s_up).wait_recv()
                send_up[s_up] = (partial(s_up) + recv_up[s_up].astype(F32)).astype(BF16)

            up_copy(s_up).start()

        t_dn = i
        s_dn = t_dn * share + k

        @pl.when(t_dn < d)
        def _():
            send_dn[s_dn] = partial(s_dn).astype(BF16)

            @pl.when(d < depth - 1)
            def _():
                dn_copy(s_dn).wait_recv()
                send_dn[s_dn] = (partial(s_dn) + recv_dn[s_dn].astype(F32)).astype(BF16)

            dn_copy(s_dn).start()

        return carry

    lax.fori_loop(0, (depth - 1) * share, z_body, 0)

    def own_body(k, carry):
        s = d * share + k
        out[0, k] = partial(s)

        @pl.when(d > 0)
        def _():
            up_copy(s).wait_recv()
            out[0, k] += recv_up[s].astype(F32)

        @pl.when(d < depth - 1)
        def _():
            dn_copy(s).wait_recv()
            out[0, k] += recv_dn[s].astype(F32)

        return carry

    lax.fori_loop(0, share, own_body, 0)

    xg.drain()
    hg.drain()
    for t in range(1, rows):
        g_copy(t).wait_send()

    def z_drain(s, carry):
        t = s // share

        @pl.when(t > d)
        def _():
            up_copy(s).wait_send()

        @pl.when(t < d)
        def _():
            dn_copy(s).wait_send()

        return carry

    lax.fori_loop(0, slots, z_drain, 0)


def body(rows, depth, node_feat, grad_out, adjacency, tile_count, tile_row, tile_col):
    slots, tile = adjacency.shape[:2]
    feat = node_feat.shape[0]
    tiles = node_feat.shape[1] // tile
    share = slots // depth
    dma = pltpu.SemaphoreType.DMA
    any_spec = pl.BlockSpec(memory_space=pl.ANY)
    smem = pl.BlockSpec(memory_space=pltpu.SMEM)
    ntiles = rows * tiles
    return pl.pallas_call(
        functools.partial(kernel, rows, depth),
        out_shape=jax.ShapeDtypeStruct((1, share, tile, tile), F32),
        in_specs=[any_spec] * 3 + [smem] * 3,
        out_specs=pl.BlockSpec(memory_space=pltpu.VMEM),
        scratch_shapes=[
            pltpu.VMEM((ntiles, feat, tile), BF16),
            pltpu.VMEM((ntiles, feat, tile), BF16),
            pltpu.VMEM((slots, tile, tile), BF16),
            pltpu.VMEM((tiles, feat, tile), BF16),
            pltpu.VMEM((tiles, tile, feat), BF16),
            pltpu.VMEM((tiles, tile, feat), BF16),
            pltpu.VMEM((slots, feat, tile), F32),
            pltpu.VMEM((rows, 2, feat, tile), BF16),
            pltpu.VMEM((rows, 2, feat, tile), BF16),
            pltpu.VMEM((tiles, feat, tile), F32),
            pltpu.VMEM((slots, tile, tile), BF16),
            pltpu.VMEM((slots, tile, tile), BF16),
            pltpu.VMEM((slots, tile, tile), BF16),
            pltpu.VMEM((slots, tile, tile), BF16),
            dma((2 * tiles + 1,)),
            dma((2 * rows,)),
            dma((2 * rows,)),
            dma((2 * rows,)),
            dma((2 * rows,)),
            dma((rows,)),
            dma((rows,)),
            dma((slots,)),
            dma((slots,)),
            dma((slots,)),
            dma((slots,)),
        ],
        compiler_params=pltpu.CompilerParams(
            collective_id=0, has_side_effects=True, vmem_limit_bytes=44 * 1024 * 1024
        ),
    )(node_feat, grad_out, adjacency, tile_count, tile_row, tile_col)


def solution(mesh):
    in_specs = (P("depth", "rows"), P("depth", "rows"), P("rows", None, None), P(), P(), P())
    out_specs = P("rows", "depth", None, None)
    call = functools.partial(body, mesh.shape["rows"], mesh.shape["depth"])
    return jax.shard_map(call, mesh=mesh, in_specs=in_specs, out_specs=out_specs, check_vma=False)
```

```python
import functools

import jax
import jax.numpy as jnp
from jax import lax
from jax.experimental import pallas as pl
from jax.experimental.pallas import tpu as pltpu
from jax.sharding import PartitionSpec as P

MESH = pl.DeviceIdType.MESH
F32 = jnp.float32
BF16 = jnp.bfloat16


def flip(index, mask):
    bit = 1
    out = index
    while bit <= mask:
        if mask & bit:
            out = out + bit * (1 - 2 * ((index // bit) % 2))
        bit *= 2
    return out


def bit_orders(rows):
    bits = []
    bit = 1
    while bit < rows:
        bits.append(bit)
        bit *= 2
    core, chip = bits[:1], bits[1:]
    half = len(chip) // 2
    x_bits, y_bits = chip[:half], chip[half:]
    return (y_bits + x_bits + core, x_bits + y_bits + core)


class Gather:
    def __init__(self, rows, tiles, buf, send_sem, recv_sem, depth_id, me):
        self.rows, self.tiles, self.buf = rows, tiles, buf
        self.send_sem, self.recv_sem = send_sem, recv_sem
        self.depth_id, self.me = depth_id, me
        self.orders = bit_orders(rows)

    def mask(self, half, place):
        out = 0
        for n, bit in enumerate(self.orders[half]):
            if place >> n & 1:
                out |= bit
        return out

    def copy(self, half, place, n):
        mask = self.mask(half, place)
        bit = self.orders[half][n]
        part = self.tiles // 2
        block = flip(self.me, mask)
        ref = self.buf.at[pl.ds(block * self.tiles + half * part, part)]
        sem = half * self.rows + (mask | bit)
        return pltpu.make_async_remote_copy(
            src_ref=ref,
            dst_ref=ref,
            send_sem=self.send_sem.at[sem],
            recv_sem=self.recv_sem.at[sem],
            device_id=(self.depth_id, flip(self.me, bit)),
            device_id_type=MESH,
        )

    def incoming(self, half, place):
        mask = self.mask(half, place)
        part = self.tiles // 2
        ref = self.buf.at[pl.ds(flip(self.me, mask) * self.tiles + half * part, part)]
        sem = half * self.rows + mask
        return pltpu.make_async_remote_copy(
            src_ref=ref,
            dst_ref=ref,
            send_sem=self.send_sem.at[sem],
            recv_sem=self.recv_sem.at[sem],
            device_id=(self.depth_id, flip(self.me, mask)),
            device_id_type=MESH,
        )

    def start(self):
        for n in range(len(self.orders[0])):
            for half in range(2):
                self.copy(half, 0, n).start()

    def forward(self, begin, end):
        count = len(self.orders[0])
        for place in range(begin, end):
            for half in range(2):
                self.incoming(half, place).wait_recv()
                for n in range(place.bit_length(), count):
                    self.copy(half, place, n).start()

    def drain(self):
        count = len(self.orders[0])
        for place in range(self.rows // 2):
            for half in range(2):
                for n in range(place.bit_length(), count):
                    self.copy(half, place, n).wait_send()


def kernel(
    rows,
    depth,
    x_hbm,
    dy_hbm,
    adj_hbm,
    cnt_hbm,
    trow_hbm,
    tcol_hbm,
    out,
    cnt,
    trow,
    tcol,
    gtab,
    xbuf,
    hbuf,
    adj,
    dyt,
    dy_t,
    g_t,
    dy_t2,
    g_t2,
    xpick,
    hpick,
    x2,
    h2,
    terms,
    gterm,
    gout,
    gin,
    gacc,
    send_up,
    send_dn,
    recv_up,
    recv_dn,
    local_sem,
    xs_sem,
    xr_sem,
    hs_sem,
    hr_sem,
    gs_sem,
    gr_sem,
    us_sem,
    ur_sem,
    ds_sem,
    dr_sem,
    feat_ssem,
    feat_rsem,
    h2s_sem,
    h2r_sem,
):
    d = lax.axis_index("depth")
    me = lax.axis_index("rows")
    feat = xbuf.shape[1]
    tile = xbuf.shape[2]
    tiles = dyt.shape[0]
    slots = adj.shape[0]
    share = slots // depth
    last_d = depth - 1
    group = 4

    x_local, dy_local = [], []
    for j in range(tiles):
        cols = pl.ds(j * tile, tile)
        x_local.append(
            pltpu.make_async_copy(x_hbm.at[:, cols], xbuf.at[me * tiles + j], local_sem.at[j])
        )
        dy_local.append(
            pltpu.make_async_copy(dy_hbm.at[:, cols], dyt.at[j], local_sem.at[tiles + j])
        )
    adj_local = pltpu.make_async_copy(adj_hbm, adj, local_sem.at[2 * tiles])
    table_local = [
        pltpu.make_async_copy(src, dst, local_sem.at[2 * tiles + 1 + n])
        for n, (src, dst) in enumerate(((cnt_hbm, cnt), (trow_hbm, trow), (tcol_hbm, tcol)))
    ]
    for c in x_local + table_local + dy_local + [adj_local]:
        c.start()

    barrier = pltpu.get_barrier_semaphore()
    for t in range(1, rows):
        pl.semaphore_signal(
            barrier, inc=1, device_id=(d, (me + t) % rows), device_id_type=MESH
        )
    for t in range(1, depth):
        pl.semaphore_signal(
            barrier, inc=1, device_id=((d + t) % depth, me), device_id_type=MESH
        )

    @pl.when(d <= 1)
    def _():
        recv_up[...] = jnp.zeros_like(recv_up)

    @pl.when(d >= last_d - 1)
    def _():
        recv_dn[...] = jnp.zeros_like(recv_dn)

    for t in range(rows):
        gin[t, 2] = jnp.zeros((feat, tile), BF16)
    gacc[...] = jnp.zeros_like(gacc)

    pl.semaphore_wait(barrier, rows - 1 + depth - 1)

    for c in x_local:
        c.wait()
    xg = Gather(rows, tiles, xbuf, xs_sem, xr_sem, d, me)
    hg = Gather(rows, tiles, hbuf, hs_sem, hr_sem, d, me)
    xg.start()
    for c in table_local + dy_local + [adj_local]:
        c.wait()

    my_count = cnt[me]

    def g_body(n, carry):
        for u in range(group):
            s = n * group + u
            g = jnp.dot(dyt[trow[me, s]], adj[s], preferred_element_type=F32)
            gterm[s] = g.astype(BF16)
        return carry

    lax.fori_loop(0, slots // group, g_body, 0)

    def g_pick(t, carry):
        o = (me + t) % rows
        first = jnp.int32(0)
        last = jnp.int32(0)
        seen = jnp.int32(0)
        for s in range(slots):
            hit = (s < my_count) & (lax.div(tcol[me, s], jnp.int32(tiles)) == o)
            last = jnp.where(hit, s, last)
            first = jnp.where(hit & (seen == 0), s, first)
            seen = jnp.where(hit, 1, seen)
        gout[t, 0] = gterm[first]
        gout[t, 1] = gterm[last]
        return carry

    lax.fori_loop(0, rows, g_pick, 0)

    def g_copy(t):
        return pltpu.make_async_remote_copy(
            src_ref=gout.at[t],
            dst_ref=gin.at[t, pl.ds(0, 2)],
            send_sem=gs_sem.at[t],
            recv_sem=gr_sem.at[t],
            device_id=(d, (me + t) % rows),
            device_id_type=MESH,
        )

    xg.forward(1, rows // 4)
    for t in range(1, rows):
        g_copy(t).start()
    gin[0, pl.ds(0, 2)] = gout[0]

    is_end = (d == 0) | (d == last_d)
    is_next = (d == 1) | (d == last_d - 1)
    inner = jnp.where(d < 2, 1 - d, 2 * last_d - 1 - d)
    inner = jnp.where(d < 2, inner, jnp.where(d >= last_d - 1, inner, 0))
    end_id = (inner, me)
    kept = (depth - 1) * share
    low = jnp.where(d < 2, share, 0)

    def feat_copy(src, dst, n):
        return pltpu.make_async_remote_copy(
            src_ref=src,
            dst_ref=dst,
            send_sem=feat_ssem.at[n],
            recv_sem=feat_rsem.at[n],
            device_id=end_id,
            device_id_type=MESH,
        )

    def dy_feat():
        return feat_copy(dy_t, dy_t2, 0)

    def x_feat():
        at = pl.ds(low, kept)
        return feat_copy(xpick.at[at], x2.at[at], 1)

    def g_feat():
        return feat_copy(g_t, g_t2, 2)

    def h_feat(s):
        return pltpu.make_async_remote_copy(
            src_ref=hpick.at[s],
            dst_ref=h2.at[s],
            send_sem=h2s_sem.at[s],
            recv_sem=h2r_sem.at[s],
            device_id=end_id,
            device_id_type=MESH,
        )

    for j in range(tiles):
        dy_t[j] = dyt[j].astype(F32).T.astype(BF16)

    @pl.when(is_end)
    def _():
        dy_feat().start()

    def g_table(t, carry):
        p = (me + rows - t) % rows
        count = cnt[p]
        seen = jnp.int32(0)
        rank = [jnp.int32(2) for _ in range(tiles)]
        for s in range(slots):
            off = tcol[p, s] - me * tiles
            off = jnp.where(s < count, off, -1)
            for j in range(tiles):
                rank[j] = jnp.where(off == j, seen, rank[j])
            seen = jnp.where((off >= 0) & (off < tiles), 1, seen)
        for j in range(tiles):
            gtab[t * tiles + j] = rank[j]
        return carry

    lax.fori_loop(0, rows, g_table, 0)

    xg.forward(rows // 4, rows)

    def h_body(n, carry):
        for u in range(group):
            s = n * group + u
            x = xbuf[tcol[me, s]]
            xpick[s] = x
            terms[s] = lax.dot_general(
                x, adj[s], (((1,), (1,)), ((), ())), preferred_element_type=F32
            )
        return carry

    lax.fori_loop(0, slots // group, h_body, 0)

    chunk = min(32, feat)

    def h_sum(c, carry):
        at = pl.ds(pl.multiple_of(c * chunk, chunk), chunk)
        total = [jnp.zeros((chunk, tile), F32) for _ in range(tiles)]
        for s in range(slots):
            term = terms[s, at, :]
            row = jnp.where(s < my_count, trow[me, s], -1)
            for i in range(tiles):
                total[i] = total[i] + jnp.where(row == i, term, 0.0)
        for i in range(tiles):
            hbuf[me * tiles + i, at, :] = total[i].astype(BF16)
        return carry

    lax.fori_loop(0, feat // chunk, h_sum, 0)
    hg.start()

    @pl.when(is_end)
    def _():
        x_feat().start()

    for t in range(1, rows):
        g_copy(t).wait_recv()

    def g_sum(t, carry):
        for j in range(tiles):
            gacc[j] += gin[t, gtab[t * tiles + j]].astype(F32)
        return carry

    lax.fori_loop(0, rows, g_sum, 0)
    for j in range(tiles):
        g_t[j] = gacc[j].astype(BF16).astype(F32).T.astype(BF16)

    @pl.when(is_end)
    def _():
        g_feat().start()

    hg.forward(1, rows)

    def up_slot(n):
        return (last_d - n // share) * share + n % share

    def h_send(n, carry):
        s = jnp.where(d == 0, up_slot(n), n)
        hpick[s] = hbuf[tcol[me, s]]
        h_feat(s).start()
        return carry

    @pl.when(is_end)
    def _():
        lax.fori_loop(0, kept, h_send, 0)

    @pl.when(is_next)
    def _():
        dy_feat().wait_recv()
        x_feat().wait_recv()
        g_feat().wait_recv()

    def dots(dy, g, h, x):
        lhs = jnp.concatenate([dy, g], axis=1)
        rhs = jnp.concatenate([h, x], axis=0)
        return jnp.dot(lhs, rhs, preferred_element_type=F32)

    def live(s, p):
        return jnp.where(s < my_count, p, 0.0)

    def partial(s):
        row = trow[me, s]
        col = tcol[me, s]
        return live(s, dots(dy_t[row], g_t[row], hbuf[col], xbuf[col]))

    def partial_end(s):
        row = trow[me, s]
        return live(s, dots(dy_t2[row], g_t2[row], h2[s], x2[s]))

    def up_copy(s):
        return pltpu.make_async_remote_copy(
            src_ref=send_up.at[s],
            dst_ref=recv_up.at[s],
            send_sem=us_sem.at[s],
            recv_sem=ur_sem.at[s],
            device_id=((d + 1) % depth, me),
            device_id_type=MESH,
        )

    def dn_copy(s):
        return pltpu.make_async_remote_copy(
            src_ref=send_dn.at[s],
            dst_ref=recv_dn.at[s],
            send_sem=ds_sem.at[s],
            recv_sem=dr_sem.at[s],
            device_id=((d + depth - 1) % depth, me),
            device_id_type=MESH,
        )

    def up_step(n):
        s = up_slot(n)

        @pl.when((d == 1) & (n < (last_d - 1) * share))
        def _():
            p = partial(s)
            h_feat(s).wait_recv()
            send_up[s] = (p + partial_end(s)).astype(BF16)
            up_copy(s).start()

        @pl.when((d > 1) & (d < last_d) & (n < (last_d - d) * share))
        def _():
            p = partial(s)
            up_copy(s).wait_recv()
            send_up[s] = (p + recv_up[s].astype(F32)).astype(BF16)
            up_copy(s).start()

    def dn_step(n):
        @pl.when((d == last_d - 1) & (n < d * share))
        def _():
            p = partial(n)
            h_feat(n).wait_recv()
            send_dn[n] = (p + partial_end(n)).astype(BF16)
            dn_copy(n).start()

        @pl.when((d > 0) & (d < last_d - 1) & (n < d * share))
        def _():
            p = partial(n)
            dn_copy(n).wait_recv()
            send_dn[n] = (p + recv_dn[n].astype(F32)).astype(BF16)
            dn_copy(n).start()

    lag = 1

    def z_body(n, carry):
        @pl.when(d < last_d - 1)
        def _():
            up_step(n)

            @pl.when(n >= lag)
            def _():
                dn_step(n - lag)

        @pl.when(d == last_d - 1)
        def _():
            dn_step(n)

            @pl.when(n >= lag)
            def _():
                up_step(n - lag)

        return carry

    @pl.when((d > 0) & (d < last_d))
    def _():
        lax.fori_loop(0, (last_d - 1) * share + lag, z_body, 0)

    def own_first(k, carry):
        out[0, k] = partial(d * share + k)
        return carry

    lax.fori_loop(0, share, own_first, 0)

    def own_end(k, carry):
        s = d * share + k
        h_feat(s).wait_recv()
        out[0, k] += partial_end(s)
        return carry

    @pl.when(is_next)
    def _():
        lax.fori_loop(0, share, own_end, 0)

    def own_up(k, carry):
        s = d * share + k
        up_copy(s).wait_recv()
        out[0, k] += recv_up[s].astype(F32)
        return carry

    def own_dn(k, carry):
        s = d * share + k
        dn_copy(s).wait_recv()
        out[0, k] += recv_dn[s].astype(F32)
        return carry

    @pl.when(d >= 2)
    def _():
        lax.fori_loop(0, share, own_up, 0)

    @pl.when(d <= last_d - 2)
    def _():
        lax.fori_loop(0, share, own_dn, 0)

    xg.drain()
    hg.drain()
    for t in range(1, rows):
        g_copy(t).wait_send()

    @pl.when(is_end)
    def _():
        dy_feat().wait_send()
        x_feat().wait_send()
        g_feat().wait_send()

        def h_drain(n, carry):
            h_feat(low + n).wait_send()
            return carry

        lax.fori_loop(0, kept, h_drain, 0)

    def z_drain(s, carry):
        t = s // share

        @pl.when((d > 0) & (d < last_d) & (t > d))
        def _():
            up_copy(s).wait_send()

        @pl.when((d > 0) & (d < last_d) & (t < d))
        def _():
            dn_copy(s).wait_send()

        return carry

    lax.fori_loop(0, slots, z_drain, 0)


def body(rows, depth, node_feat, grad_out, adjacency, tile_count, tile_row, tile_col):
    slots, tile = adjacency.shape[:2]
    feat = node_feat.shape[0]
    tiles = node_feat.shape[1] // tile
    share = slots // depth
    dma = pltpu.SemaphoreType.DMA
    hbm = pl.BlockSpec(memory_space=pltpu.HBM)
    ntiles = rows * tiles
    node = pltpu.VMEM((ntiles, feat, tile), BF16)
    turned = pltpu.VMEM((tiles, tile, feat), BF16)
    picked = pltpu.VMEM((slots, feat, tile), BF16)
    sums = pltpu.VMEM((slots, tile, tile), BF16)
    return pl.pallas_call(
        functools.partial(kernel, rows, depth),
        out_shape=jax.ShapeDtypeStruct((1, share, tile, tile), F32),
        in_specs=[hbm] * 6,
        out_specs=pl.BlockSpec(memory_space=pltpu.VMEM),
        scratch_shapes=[
            pltpu.SMEM(tile_count.shape, jnp.int32),
            pltpu.SMEM(tile_row.shape, jnp.int32),
            pltpu.SMEM(tile_col.shape, jnp.int32),
            pltpu.SMEM((rows * tiles,), jnp.int32),
            node,
            node,
            sums,
            pltpu.VMEM((tiles, feat, tile), BF16),
            turned,
            turned,
            turned,
            turned,
            picked,
            picked,
            picked,
            picked,
            pltpu.VMEM((slots, feat, tile), F32),
            picked,
            pltpu.VMEM((rows, 2, feat, tile), BF16),
            pltpu.VMEM((rows, 3, feat, tile), BF16),
            pltpu.VMEM((tiles, feat, tile), F32),
            sums,
            sums,
            sums,
            sums,
            dma((2 * tiles + 4,)),
            dma((2 * rows,)),
            dma((2 * rows,)),
            dma((2 * rows,)),
            dma((2 * rows,)),
            dma((rows,)),
            dma((rows,)),
            dma((slots,)),
            dma((slots,)),
            dma((slots,)),
            dma((slots,)),
            dma((3,)),
            dma((3,)),
            dma((slots,)),
            dma((slots,)),
        ],
        compiler_params=pltpu.CompilerParams(
            collective_id=0, has_side_effects=True, vmem_limit_bytes=48 * 1024 * 1024
        ),
    )(node_feat, grad_out, adjacency, tile_count, tile_row, tile_col)


def solution(mesh):
    in_specs = (P("depth", "rows"), P("depth", "rows"), P("rows", None, None), P(), P(), P())
    out_specs = P("rows", "depth", None, None)
    call = functools.partial(body, mesh.shape["rows"], mesh.shape["depth"])
    return jax.shard_map(call, mesh=mesh, in_specs=in_specs, out_specs=out_specs, check_vma=False)
```

```python
import functools

import jax
import jax.numpy as jnp
from jax import lax
from jax.experimental import pallas as pl
from jax.experimental.pallas import tpu as pltpu
from jax.sharding import PartitionSpec as P

MESH = pl.DeviceIdType.MESH
F32 = jnp.float32
BF16 = jnp.bfloat16


def flip(index, mask):
    bit = 1
    out = index
    while bit <= mask:
        if mask & bit:
            out = out + bit * (1 - 2 * ((index // bit) % 2))
        bit *= 2
    return out


def bit_orders(rows):
    bits = []
    bit = 1
    while bit < rows:
        bits.append(bit)
        bit *= 2
    core, chip = bits[:1], bits[1:]
    half = len(chip) // 2
    x_bits, y_bits = chip[:half], chip[half:]
    return (y_bits + x_bits + core, x_bits + y_bits + core)


def peer(index, mask, bits):
    out = index
    for bit in bits:
        out = out + bit * (1 - 2 * ((index // bit) % 2)) * ((mask // bit) % 2)
    return out


class Gather:
    def __init__(self, rows, tiles, buf, send_sem, recv_sem, depth_id, me):
        self.rows, self.tiles, self.buf = rows, tiles, buf
        self.send_sem, self.recv_sem = send_sem, recv_sem
        self.depth_id, self.me = depth_id, me
        self.orders = bit_orders(rows)

    def mask(self, half, place):
        out = 0
        for n, bit in enumerate(self.orders[half]):
            if place >> n & 1:
                out |= bit
        return out

    def copy(self, half, place, n):
        mask = self.mask(half, place)
        bit = self.orders[half][n]
        part = self.tiles // 2
        block = flip(self.me, mask)
        ref = self.buf.at[pl.ds(block * self.tiles + half * part, part)]
        sem = half * self.rows + (mask | bit)
        return pltpu.make_async_remote_copy(
            src_ref=ref,
            dst_ref=ref,
            send_sem=self.send_sem.at[sem],
            recv_sem=self.recv_sem.at[sem],
            device_id=(self.depth_id, flip(self.me, bit)),
            device_id_type=MESH,
        )

    def incoming(self, half, place):
        mask = self.mask(half, place)
        part = self.tiles // 2
        ref = self.buf.at[pl.ds(flip(self.me, mask) * self.tiles + half * part, part)]
        sem = half * self.rows + mask
        return pltpu.make_async_remote_copy(
            src_ref=ref,
            dst_ref=ref,
            send_sem=self.send_sem.at[sem],
            recv_sem=self.recv_sem.at[sem],
            device_id=(self.depth_id, flip(self.me, mask)),
            device_id_type=MESH,
        )

    def start(self):
        for n in range(len(self.orders[0])):
            for half in range(2):
                self.copy(half, 0, n).start()

    def forward(self, begin, end):
        count = len(self.orders[0])
        for place in range(begin, end):
            for half in range(2):
                self.incoming(half, place).wait_recv()
                for n in range(place.bit_length(), count):
                    self.copy(half, place, n).start()

    def drain(self):
        count = len(self.orders[0])
        for place in range(self.rows // 2):
            for half in range(2):
                for n in range(place.bit_length(), count):
                    self.copy(half, place, n).wait_send()


def kernel(
    rows,
    depth,
    x_hbm,
    dy_hbm,
    adj_hbm,
    cnt_hbm,
    trow_hbm,
    tcol_hbm,
    out_hbm,
    out,
    cnt,
    trow,
    tcol,
    gtab,
    xbuf,
    hbuf,
    adj,
    dyt,
    dy_t,
    g_t,
    dy_t2,
    g_t2,
    xpick,
    hpick,
    x2,
    h2,
    terms,
    gterm,
    gout,
    gin,
    gacc,
    send_up,
    send_dn,
    recv_up,
    recv_dn,
    local_sem,
    xs_sem,
    xr_sem,
    hs_sem,
    hr_sem,
    gs_sem,
    gr_sem,
    us_sem,
    ur_sem,
    ds_sem,
    dr_sem,
    feat_ssem,
    feat_rsem,
    h2s_sem,
    h2r_sem,
):
    d = lax.axis_index("depth")
    me = lax.axis_index("rows")
    feat = xbuf.shape[1]
    tile = xbuf.shape[2]
    tiles = dyt.shape[0]
    slots = adj.shape[0]
    share = slots // depth
    last_d = depth - 1
    group = 4
    bits = sorted(bit_orders(rows)[0])

    x_local, dy_local = [], []
    for j in range(tiles):
        cols = pl.ds(j * tile, tile)
        x_local.append(
            pltpu.make_async_copy(x_hbm.at[:, cols], xbuf.at[me * tiles + j], local_sem.at[j])
        )
        dy_local.append(
            pltpu.make_async_copy(dy_hbm.at[:, cols], dyt.at[j], local_sem.at[tiles + j])
        )
    adj_local = pltpu.make_async_copy(adj_hbm, adj, local_sem.at[2 * tiles])
    table_local = [
        pltpu.make_async_copy(src, dst, local_sem.at[2 * tiles + 1 + n])
        for n, (src, dst) in enumerate(((cnt_hbm, cnt), (trow_hbm, trow), (tcol_hbm, tcol)))
    ]
    for c in x_local + table_local + dy_local + [adj_local]:
        c.start()

    barrier = pltpu.get_barrier_semaphore()
    for t in range(1, rows):
        pl.semaphore_signal(
            barrier, inc=1, device_id=(d, (me + t) % rows), device_id_type=MESH
        )
    for t in range(1, depth):
        pl.semaphore_signal(
            barrier, inc=1, device_id=((d + t) % depth, me), device_id_type=MESH
        )

    @pl.when(d <= 1)
    def _():
        recv_up[...] = jnp.zeros_like(recv_up)

    @pl.when(d >= last_d - 1)
    def _():
        recv_dn[...] = jnp.zeros_like(recv_dn)

    for t in range(rows):
        gin[t, 2] = jnp.zeros((feat, tile), BF16)
    gacc[...] = jnp.zeros_like(gacc)

    pl.semaphore_wait(barrier, rows - 1 + depth - 1)

    for c in x_local:
        c.wait()
    xg = Gather(rows, tiles, xbuf, xs_sem, xr_sem, d, me)
    hg = Gather(rows, tiles, hbuf, hs_sem, hr_sem, d, me)
    xg.start()
    for c in table_local + dy_local + [adj_local]:
        c.wait()

    my_count = cnt[me]

    def g_body(n, carry):
        for u in range(group):
            s = n * group + u
            g = jnp.dot(dyt[trow[me, s]], adj[s], preferred_element_type=F32)
            gterm[s] = g.astype(BF16)
        return carry

    lax.fori_loop(0, slots // group, g_body, 0)

    def g_pick(t, carry):
        o = peer(me, t, bits)
        first = jnp.int32(0)
        last = jnp.int32(0)
        seen = jnp.int32(0)
        for s in range(slots):
            hit = (s < my_count) & (lax.div(tcol[me, s], jnp.int32(tiles)) == o)
            last = jnp.where(hit, s, last)
            first = jnp.where(hit & (seen == 0), s, first)
            seen = jnp.where(hit, 1, seen)
        gout[t, 0] = gterm[first]
        gout[t, 1] = gterm[last]
        return carry

    lax.fori_loop(0, rows, g_pick, 0)

    def g_copy(t):
        return pltpu.make_async_remote_copy(
            src_ref=gout.at[t],
            dst_ref=gin.at[t, pl.ds(0, 2)],
            send_sem=gs_sem.at[t],
            recv_sem=gr_sem.at[t],
            device_id=(d, flip(me, t)),
            device_id_type=MESH,
        )

    xg.forward(1, rows // 4)
    order = sorted(range(1, rows), key=lambda t: (-bin(t // 2).count("1"), t % 2, t))
    for t in order:
        g_copy(t).start()
    gin[0, pl.ds(0, 2)] = gout[0]

    is_end = (d == 0) | (d == last_d)
    is_next = (d == 1) | (d == last_d - 1)
    inner = jnp.where(d < 2, 1 - d, 2 * last_d - 1 - d)
    inner = jnp.where(d < 2, inner, jnp.where(d >= last_d - 1, inner, 0))
    end_id = (inner, me)
    kept = (depth - 1) * share
    low = jnp.where(d < 2, share, 0)

    def feat_copy(src, dst, n):
        return pltpu.make_async_remote_copy(
            src_ref=src,
            dst_ref=dst,
            send_sem=feat_ssem.at[n],
            recv_sem=feat_rsem.at[n],
            device_id=end_id,
            device_id_type=MESH,
        )

    def dy_feat():
        return feat_copy(dy_t, dy_t2, 0)

    def x_feat():
        at = pl.ds(low, kept)
        return feat_copy(xpick.at[at], x2.at[at], 1)

    def g_feat():
        return feat_copy(g_t, g_t2, 2)

    def h_feat(s):
        return pltpu.make_async_remote_copy(
            src_ref=hpick.at[s],
            dst_ref=h2.at[s],
            send_sem=h2s_sem.at[s],
            recv_sem=h2r_sem.at[s],
            device_id=end_id,
            device_id_type=MESH,
        )

    for j in range(tiles):
        dy_t[j] = dyt[j].astype(F32).T.astype(BF16)

    @pl.when(is_end)
    def _():
        dy_feat().start()

    def g_table(t, carry):
        p = peer(me, t, bits)
        count = cnt[p]
        seen = jnp.int32(0)
        rank = [jnp.int32(2) for _ in range(tiles)]
        for s in range(slots):
            off = tcol[p, s] - me * tiles
            off = jnp.where(s < count, off, -1)
            for j in range(tiles):
                rank[j] = jnp.where(off == j, seen, rank[j])
            seen = jnp.where((off >= 0) & (off < tiles), 1, seen)
        for j in range(tiles):
            gtab[t * tiles + j] = rank[j]
        return carry

    lax.fori_loop(0, rows, g_table, 0)

    xg.forward(rows // 4, rows)

    def h_body(n, carry):
        for u in range(group):
            s = n * group + u
            x = xbuf[tcol[me, s]]
            xpick[s] = x
            terms[s] = lax.dot_general(
                x, adj[s], (((1,), (1,)), ((), ())), preferred_element_type=F32
            )
        return carry

    lax.fori_loop(0, slots // group, h_body, 0)

    chunk = min(32, feat)

    def h_sum(c, carry):
        at = pl.ds(pl.multiple_of(c * chunk, chunk), chunk)
        total = [jnp.zeros((chunk, tile), F32) for _ in range(tiles)]
        for s in range(slots):
            term = terms[s, at, :]
            row = jnp.where(s < my_count, trow[me, s], -1)
            for i in range(tiles):
                total[i] = total[i] + jnp.where(row == i, term, 0.0)
        for i in range(tiles):
            hbuf[me * tiles + i, at, :] = total[i].astype(BF16)
        return carry

    lax.fori_loop(0, feat // chunk, h_sum, 0)
    hg.start()

    @pl.when(is_end)
    def _():
        x_feat().start()

    hg.forward(1, rows // 4)
    for t in range(1, rows):
        g_copy(t).wait_recv()

    def g_sum(t, carry):
        for j in range(tiles):
            gacc[j] += gin[t, gtab[t * tiles + j]].astype(F32)
        return carry

    lax.fori_loop(0, rows, g_sum, 0)
    for j in range(tiles):
        g_t[j] = gacc[j].astype(BF16).astype(F32).T.astype(BF16)

    @pl.when(is_end)
    def _():
        g_feat().start()

    hg.forward(rows // 4, rows)

    def up_slot(n):
        return (last_d - n // share) * share + n % share

    def h_send(n, carry):
        s = jnp.where(d == 0, up_slot(n), n)
        hpick[s] = hbuf[tcol[me, s]]
        h_feat(s).start()
        return carry

    @pl.when(is_end)
    def _():
        lax.fori_loop(0, kept, h_send, 0)

    @pl.when(is_next)
    def _():
        dy_feat().wait_recv()
        x_feat().wait_recv()
        g_feat().wait_recv()

    def dots(dy, g, h, x):
        lhs = jnp.concatenate([dy, g], axis=1)
        rhs = jnp.concatenate([h, x], axis=0)
        return jnp.dot(lhs, rhs, preferred_element_type=F32)

    def live(s, p):
        return jnp.where(s < my_count, p, 0.0)

    def partial(s):
        row = trow[me, s]
        col = tcol[me, s]
        return live(s, dots(dy_t[row], g_t[row], hbuf[col], xbuf[col]))

    def partial_end(s):
        row = trow[me, s]
        return live(s, dots(dy_t2[row], g_t2[row], h2[s], x2[s]))

    def up_copy(s):
        return pltpu.make_async_remote_copy(
            src_ref=send_up.at[s],
            dst_ref=recv_up.at[s],
            send_sem=us_sem.at[s],
            recv_sem=ur_sem.at[s],
            device_id=((d + 1) % depth, me),
            device_id_type=MESH,
        )

    def dn_copy(s):
        return pltpu.make_async_remote_copy(
            src_ref=send_dn.at[s],
            dst_ref=recv_dn.at[s],
            send_sem=ds_sem.at[s],
            recv_sem=dr_sem.at[s],
            device_id=((d + depth - 1) % depth, me),
            device_id_type=MESH,
        )

    def up_step(n):
        s = up_slot(n)

        @pl.when((d == 1) & (n < (last_d - 1) * share))
        def _():
            p = partial(s)
            h_feat(s).wait_recv()
            send_up[s] = (p + partial_end(s)).astype(BF16)
            up_copy(s).start()

        @pl.when((d > 1) & (d < last_d) & (n < (last_d - d) * share))
        def _():
            p = partial(s)
            up_copy(s).wait_recv()
            send_up[s] = (p + recv_up[s].astype(F32)).astype(BF16)
            up_copy(s).start()

    def dn_step(n):
        @pl.when((d == last_d - 1) & (n < d * share))
        def _():
            p = partial(n)
            h_feat(n).wait_recv()
            send_dn[n] = (p + partial_end(n)).astype(BF16)
            dn_copy(n).start()

        @pl.when((d > 0) & (d < last_d - 1) & (n < d * share))
        def _():
            p = partial(n)
            dn_copy(n).wait_recv()
            send_dn[n] = (p + recv_dn[n].astype(F32)).astype(BF16)
            dn_copy(n).start()

    lag = 1

    def z_body(n, carry):
        @pl.when(d < last_d - 1)
        def _():
            up_step(n)

            @pl.when(n >= lag)
            def _():
                dn_step(n - lag)

        @pl.when(d == last_d - 1)
        def _():
            dn_step(n)

            @pl.when(n >= lag)
            def _():
                up_step(n - lag)

        return carry

    @pl.when((d > 0) & (d < last_d))
    def _():
        lax.fori_loop(0, (last_d - 1) * share + lag, z_body, 0)

    def own_first(k, carry):
        out[k] = partial(d * share + k)
        return carry

    lax.fori_loop(0, share, own_first, 0)

    def own_end(k, carry):
        s = d * share + k
        h_feat(s).wait_recv()
        out[k] += partial_end(s)
        return carry

    @pl.when(is_next)
    def _():
        lax.fori_loop(0, share, own_end, 0)

    def own_up(k, carry):
        s = d * share + k
        up_copy(s).wait_recv()
        out[k] += recv_up[s].astype(F32)
        return carry

    def own_dn(k, carry):
        s = d * share + k
        dn_copy(s).wait_recv()
        out[k] += recv_dn[s].astype(F32)
        return carry

    @pl.when(d >= 2)
    def _():
        lax.fori_loop(0, share, own_up, 0)

    @pl.when(d <= last_d - 2)
    def _():
        lax.fori_loop(0, share, own_dn, 0)

    result = pltpu.make_async_copy(out, out_hbm.at[0], local_sem.at[2 * tiles + 4])
    result.start()
    xg.drain()
    hg.drain()
    for t in range(1, rows):
        g_copy(t).wait_send()

    @pl.when(is_end)
    def _():
        dy_feat().wait_send()
        x_feat().wait_send()
        g_feat().wait_send()

        def h_drain(n, carry):
            h_feat(low + n).wait_send()
            return carry

        lax.fori_loop(0, kept, h_drain, 0)

    def z_drain(s, carry):
        t = s // share

        @pl.when((d > 0) & (d < last_d) & (t > d))
        def _():
            up_copy(s).wait_send()

        @pl.when((d > 0) & (d < last_d) & (t < d))
        def _():
            dn_copy(s).wait_send()

        return carry

    lax.fori_loop(0, slots, z_drain, 0)
    result.wait()


def body(rows, depth, node_feat, grad_out, adjacency, tile_count, tile_row, tile_col):
    slots, tile = adjacency.shape[:2]
    feat = node_feat.shape[0]
    tiles = node_feat.shape[1] // tile
    share = slots // depth
    dma = pltpu.SemaphoreType.DMA
    hbm = pl.BlockSpec(memory_space=pltpu.HBM)
    ntiles = rows * tiles
    node = pltpu.VMEM((ntiles, feat, tile), BF16)
    turned = pltpu.VMEM((tiles, tile, feat), BF16)
    picked = pltpu.VMEM((slots, feat, tile), BF16)
    sums = pltpu.VMEM((slots, tile, tile), BF16)
    return pl.pallas_call(
        functools.partial(kernel, rows, depth),
        out_shape=jax.ShapeDtypeStruct((1, share, tile, tile), F32),
        in_specs=[hbm] * 6,
        out_specs=hbm,
        scratch_shapes=[
            pltpu.VMEM((share, tile, tile), F32),
            pltpu.SMEM(tile_count.shape, jnp.int32),
            pltpu.SMEM(tile_row.shape, jnp.int32),
            pltpu.SMEM(tile_col.shape, jnp.int32),
            pltpu.SMEM((rows * tiles,), jnp.int32),
            node,
            node,
            sums,
            pltpu.VMEM((tiles, feat, tile), BF16),
            turned,
            turned,
            turned,
            turned,
            picked,
            picked,
            picked,
            picked,
            pltpu.VMEM((slots, feat, tile), F32),
            picked,
            pltpu.VMEM((rows, 2, feat, tile), BF16),
            pltpu.VMEM((rows, 3, feat, tile), BF16),
            pltpu.VMEM((tiles, feat, tile), F32),
            sums,
            sums,
            sums,
            sums,
            dma((2 * tiles + 5,)),
            dma((2 * rows,)),
            dma((2 * rows,)),
            dma((2 * rows,)),
            dma((2 * rows,)),
            dma((rows,)),
            dma((rows,)),
            dma((slots,)),
            dma((slots,)),
            dma((slots,)),
            dma((slots,)),
            dma((3,)),
            dma((3,)),
            dma((slots,)),
            dma((slots,)),
        ],
        compiler_params=pltpu.CompilerParams(
            collective_id=0, has_side_effects=True, vmem_limit_bytes=64 * 1024 * 1024
        ),
    )(node_feat, grad_out, adjacency, tile_count, tile_row, tile_col)


def solution(mesh):
    in_specs = (P("depth", "rows"), P("depth", "rows"), P("rows", None, None), P(), P(), P())
    out_specs = P("rows", "depth", None, None)
    call = functools.partial(body, mesh.shape["rows"], mesh.shape["depth"])
    return jax.shard_map(call, mesh=mesh, in_specs=in_specs, out_specs=out_specs, check_vma=False)
```

```python
import functools

import jax
import jax.numpy as jnp
from jax import lax
from jax.experimental import pallas as pl
from jax.experimental.pallas import tpu as pltpu
from jax.sharding import PartitionSpec as P

MESH = pl.DeviceIdType.MESH
F32 = jnp.float32
BF16 = jnp.bfloat16


def flip(index, mask):
    bit = 1
    out = index
    while bit <= mask:
        if mask & bit:
            out = out + bit * (1 - 2 * ((index // bit) % 2))
        bit *= 2
    return out


def bit_orders(rows):
    bits = []
    bit = 1
    while bit < rows:
        bits.append(bit)
        bit *= 2
    core, chip = bits[:1], bits[1:]
    half = len(chip) // 2
    x_bits, y_bits = chip[:half], chip[half:]
    return (y_bits + x_bits + core, x_bits + y_bits + core)


def peer(index, mask, bits):
    out = index
    for bit in bits:
        out = out + bit * (1 - 2 * ((index // bit) % 2)) * ((mask // bit) % 2)
    return out


class Gather:
    def __init__(self, rows, tiles, buf, send_sem, recv_sem, depth_id, me):
        self.rows, self.tiles, self.buf = rows, tiles, buf
        self.send_sem, self.recv_sem = send_sem, recv_sem
        self.depth_id, self.me = depth_id, me
        self.orders = bit_orders(rows)

    def mask(self, half, place):
        out = 0
        for n, bit in enumerate(self.orders[half]):
            if place >> n & 1:
                out |= bit
        return out

    def copy(self, half, place, n):
        mask = self.mask(half, place)
        bit = self.orders[half][n]
        part = self.tiles // 2
        block = flip(self.me, mask)
        ref = self.buf.at[pl.ds(block * self.tiles + half * part, part)]
        sem = half * self.rows + (mask | bit)
        return pltpu.make_async_remote_copy(
            src_ref=ref,
            dst_ref=ref,
            send_sem=self.send_sem.at[sem],
            recv_sem=self.recv_sem.at[sem],
            device_id=(self.depth_id, flip(self.me, bit)),
            device_id_type=MESH,
        )

    def incoming(self, half, place):
        mask = self.mask(half, place)
        part = self.tiles // 2
        ref = self.buf.at[pl.ds(flip(self.me, mask) * self.tiles + half * part, part)]
        sem = half * self.rows + mask
        return pltpu.make_async_remote_copy(
            src_ref=ref,
            dst_ref=ref,
            send_sem=self.send_sem.at[sem],
            recv_sem=self.recv_sem.at[sem],
            device_id=(self.depth_id, flip(self.me, mask)),
            device_id_type=MESH,
        )

    def start(self):
        for n in range(len(self.orders[0])):
            for half in range(2):
                self.copy(half, 0, n).start()

    def forward(self, begin, end):
        count = len(self.orders[0])
        for place in range(begin, end):
            for half in range(2):
                self.incoming(half, place).wait_recv()
                for n in range(place.bit_length(), count):
                    self.copy(half, place, n).start()

    def drain(self):
        count = len(self.orders[0])
        for place in range(self.rows // 2):
            for half in range(2):
                for n in range(place.bit_length(), count):
                    self.copy(half, place, n).wait_send()


def kernel(
    rows,
    depth,
    x_hbm,
    dy_hbm,
    adj_hbm,
    cnt_hbm,
    trow_hbm,
    tcol_hbm,
    out_hbm,
    out,
    cnt,
    trow,
    tcol,
    gtab,
    xbuf,
    hbuf_a,
    hbuf_b,
    adj,
    dyt,
    dy_t,
    g_t,
    dy_t2,
    g_t2,
    xpick,
    hpick,
    x2,
    h2,
    terms,
    gterm,
    gout,
    gin,
    gacc,
    send_up,
    send_dn,
    recv_up,
    recv_dn,
    local_sem,
    xs_sem,
    xr_sem,
    hs_sem,
    hr_sem,
    gs_sem,
    gr_sem,
    us_sem,
    ur_sem,
    ds_sem,
    dr_sem,
    feat_ssem,
    feat_rsem,
    h2s_sem,
    h2r_sem,
):
    d = lax.axis_index("depth")
    me = lax.axis_index("rows")
    feat = xbuf.shape[1]
    tile = xbuf.shape[2]
    tiles = dyt.shape[0]
    slots = adj.shape[0]
    share = slots // depth
    last_d = depth - 1
    group = 4
    bits = sorted(bit_orders(rows)[0])

    x_local, dy_local = [], []
    for j in range(tiles):
        cols = pl.ds(j * tile, tile)
        x_local.append(
            pltpu.make_async_copy(x_hbm.at[:, cols], xbuf.at[me * tiles + j], local_sem.at[j])
        )
        dy_local.append(
            pltpu.make_async_copy(dy_hbm.at[:, cols], dyt.at[j], local_sem.at[tiles + j])
        )
    adj_local = pltpu.make_async_copy(adj_hbm, adj, local_sem.at[2 * tiles])
    table_local = [
        pltpu.make_async_copy(src, dst, local_sem.at[2 * tiles + 1 + n])
        for n, (src, dst) in enumerate(((cnt_hbm, cnt), (trow_hbm, trow), (tcol_hbm, tcol)))
    ]
    for c in x_local + table_local + dy_local + [adj_local]:
        c.start()

    barrier = pltpu.get_barrier_semaphore()
    for t in range(1, rows):
        pl.semaphore_signal(
            barrier, inc=1, device_id=(d, (me + t) % rows), device_id_type=MESH
        )
    for t in range(1, depth):
        pl.semaphore_signal(
            barrier, inc=1, device_id=((d + t) % depth, me), device_id_type=MESH
        )

    @pl.when(d <= 1)
    def _():
        recv_up[...] = jnp.zeros_like(recv_up)

    @pl.when(d >= last_d - 1)
    def _():
        recv_dn[...] = jnp.zeros_like(recv_dn)

    for t in range(rows):
        gin[t, 2] = jnp.zeros((feat, tile), BF16)
    gacc[...] = jnp.zeros_like(gacc)

    pl.semaphore_wait(barrier, rows - 1 + depth - 1)

    for c in x_local:
        c.wait()
    xg = Gather(rows, tiles, xbuf, xs_sem, xr_sem, d, me)
    hbuf = (hbuf_a, hbuf_b)
    hg = [Gather(rows, tiles, hbuf[c], hs_sem.at[c], hr_sem.at[c], d, me) for c in range(2)]
    half = tile // 2
    xg.start()
    for c in table_local + dy_local + [adj_local]:
        c.wait()

    my_count = cnt[me]

    def g_body(n, carry):
        for u in range(group):
            s = n * group + u
            g = jnp.dot(dyt[trow[me, s]], adj[s], preferred_element_type=F32)
            gterm[s] = g.astype(BF16)
        return carry

    lax.fori_loop(0, slots // group, g_body, 0)

    def g_pick(t, carry):
        o = peer(me, t, bits)
        first = jnp.int32(0)
        last = jnp.int32(0)
        seen = jnp.int32(0)
        for s in range(slots):
            hit = (s < my_count) & (lax.div(tcol[me, s], jnp.int32(tiles)) == o)
            last = jnp.where(hit, s, last)
            first = jnp.where(hit & (seen == 0), s, first)
            seen = jnp.where(hit, 1, seen)
        gout[t, 0] = gterm[first]
        gout[t, 1] = gterm[last]
        return carry

    lax.fori_loop(0, rows, g_pick, 0)

    def g_copy(t):
        return pltpu.make_async_remote_copy(
            src_ref=gout.at[t],
            dst_ref=gin.at[t, pl.ds(0, 2)],
            send_sem=gs_sem.at[t],
            recv_sem=gr_sem.at[t],
            device_id=(d, flip(me, t)),
            device_id_type=MESH,
        )

    xg.forward(1, rows // 4)
    order = sorted(range(1, rows), key=lambda t: (-bin(t // 2).count("1"), t % 2, t))
    for t in order:
        g_copy(t).start()
    gin[0, pl.ds(0, 2)] = gout[0]

    is_end = (d == 0) | (d == last_d)
    is_next = (d == 1) | (d == last_d - 1)
    inner = jnp.where(d < 2, 1 - d, 2 * last_d - 1 - d)
    inner = jnp.where(d < 2, inner, jnp.where(d >= last_d - 1, inner, 0))
    end_id = (inner, me)
    kept = (depth - 1) * share
    low = jnp.where(d < 2, share, 0)

    def feat_copy(src, dst, n):
        return pltpu.make_async_remote_copy(
            src_ref=src,
            dst_ref=dst,
            send_sem=feat_ssem.at[n],
            recv_sem=feat_rsem.at[n],
            device_id=end_id,
            device_id_type=MESH,
        )

    def dy_feat():
        return feat_copy(dy_t, dy_t2, 0)

    def x_feat():
        at = pl.ds(low, kept)
        return feat_copy(xpick.at[at], x2.at[at], 1)

    def g_feat():
        return feat_copy(g_t, g_t2, 2)

    def h_feat(s):
        return pltpu.make_async_remote_copy(
            src_ref=hpick.at[s],
            dst_ref=h2.at[s],
            send_sem=h2s_sem.at[s],
            recv_sem=h2r_sem.at[s],
            device_id=end_id,
            device_id_type=MESH,
        )

    for j in range(tiles):
        dy_t[j] = dyt[j].astype(F32).T.astype(BF16)

    @pl.when(is_end)
    def _():
        dy_feat().start()

    def g_table(t, carry):
        p = peer(me, t, bits)
        count = cnt[p]
        seen = jnp.int32(0)
        rank = [jnp.int32(2) for _ in range(tiles)]
        for s in range(slots):
            off = tcol[p, s] - me * tiles
            off = jnp.where(s < count, off, -1)
            for j in range(tiles):
                rank[j] = jnp.where(off == j, seen, rank[j])
            seen = jnp.where((off >= 0) & (off < tiles), 1, seen)
        for j in range(tiles):
            gtab[t * tiles + j] = rank[j]
        return carry

    lax.fori_loop(0, rows, g_table, 0)

    xg.forward(rows // 4, rows)

    def h_body(n, carry):
        for u in range(group):
            s = n * group + u
            x = xbuf[tcol[me, s]]
            xpick[s] = x
            terms[s] = lax.dot_general(
                x, adj[s], (((1,), (1,)), ((), ())), preferred_element_type=F32
            )
        return carry

    lax.fori_loop(0, slots // group, h_body, 0)

    @pl.when(is_end)
    def _():
        x_feat().start()

    chunk = min(32, feat)

    def h_sum(c, n, carry):
        at = pl.ds(pl.multiple_of(n * chunk, chunk), chunk)
        total = [jnp.zeros((chunk, half), F32) for _ in range(tiles)]
        for s in range(slots):
            term = terms[s, at, c * half : (c + 1) * half]
            row = jnp.where(s < my_count, trow[me, s], -1)
            for i in range(tiles):
                total[i] = total[i] + jnp.where(row == i, term, 0.0)
        for i in range(tiles):
            hbuf[c][me * tiles + i, at, :] = total[i].astype(BF16)
        return carry

    for c in range(2):
        lax.fori_loop(0, feat // chunk, functools.partial(h_sum, c), 0)
        hg[c].start()
        hg[c].forward(1, rows // 4)

    for t in range(1, rows):
        g_copy(t).wait_recv()

    def g_sum(t, carry):
        for j in range(tiles):
            gacc[j] += gin[t, gtab[t * tiles + j]].astype(F32)
        return carry

    lax.fori_loop(0, rows, g_sum, 0)
    for j in range(tiles):
        g_t[j] = gacc[j].astype(BF16).astype(F32).T.astype(BF16)

    @pl.when(is_end)
    def _():
        g_feat().start()

    hg[0].forward(rows // 4, rows)

    def up_slot(n):
        return (last_d - n // share) * share + n % share

    def h_send(c, n, carry):
        s = jnp.where(d == 0, up_slot(n), n)
        hpick[c * slots + s] = hbuf[c][tcol[me, s]]
        h_feat(c * slots + s).start()
        return carry

    @pl.when(is_end)
    def _():
        lax.fori_loop(0, kept, functools.partial(h_send, 0), 0)

    @pl.when(is_next)
    def _():
        dy_feat().wait_recv()
        x_feat().wait_recv()
        g_feat().wait_recv()

    def dots(dy, g, h, x):
        lhs = jnp.concatenate([dy, g], axis=1)
        rhs = jnp.concatenate([h, x], axis=0)
        return jnp.dot(lhs, rhs, preferred_element_type=F32)

    def live(s, p):
        return jnp.where(s < my_count, p, 0.0)

    def partial(s, c):
        row = trow[me, s]
        col = tcol[me, s]
        x = xbuf[col, :, c * half : (c + 1) * half]
        return live(s, dots(dy_t[row], g_t[row], hbuf[c][col], x))

    def partial_end(s, c):
        row = trow[me, s]
        x = x2[s, :, c * half : (c + 1) * half]
        return live(s, dots(dy_t2[row], g_t2[row], h2[c * slots + s], x))

    def up_copy(s):
        return pltpu.make_async_remote_copy(
            src_ref=send_up.at[s],
            dst_ref=recv_up.at[s],
            send_sem=us_sem.at[s],
            recv_sem=ur_sem.at[s],
            device_id=((d + 1) % depth, me),
            device_id_type=MESH,
        )

    def dn_copy(s):
        return pltpu.make_async_remote_copy(
            src_ref=send_dn.at[s],
            dst_ref=recv_dn.at[s],
            send_sem=ds_sem.at[s],
            recv_sem=dr_sem.at[s],
            device_id=((d + depth - 1) % depth, me),
            device_id_type=MESH,
        )

    def up_step(n, c):
        s = up_slot(n)
        at = c * slots + s

        @pl.when((d == 1) & (n < (last_d - 1) * share))
        def _():
            p = partial(s, c)
            h_feat(at).wait_recv()
            send_up[at] = (p + partial_end(s, c)).astype(BF16)
            up_copy(at).start()

        @pl.when((d > 1) & (d < last_d) & (n < (last_d - d) * share))
        def _():
            p = partial(s, c)
            up_copy(at).wait_recv()
            send_up[at] = (p + recv_up[at].astype(F32)).astype(BF16)
            up_copy(at).start()

    def dn_step(n, c):
        at = c * slots + n

        @pl.when((d == last_d - 1) & (n < d * share))
        def _():
            p = partial(n, c)
            h_feat(at).wait_recv()
            send_dn[at] = (p + partial_end(n, c)).astype(BF16)
            dn_copy(at).start()

        @pl.when((d > 0) & (d < last_d - 1) & (n < d * share))
        def _():
            p = partial(n, c)
            dn_copy(at).wait_recv()
            send_dn[at] = (p + recv_dn[at].astype(F32)).astype(BF16)
            dn_copy(at).start()

    lag = 1

    def z_body(c, n, carry):
        @pl.when(d < last_d - 1)
        def _():
            up_step(n, c)

            @pl.when(n >= lag)
            def _():
                dn_step(n - lag, c)

        @pl.when(d == last_d - 1)
        def _():
            dn_step(n, c)

            @pl.when(n >= lag)
            def _():
                up_step(n - lag, c)

        return carry

    z_end = (last_d - 1) * share + lag
    z_mid = z_end // 2
    is_inner = (d > 0) & (d < last_d)

    @pl.when(is_inner)
    def _():
        lax.fori_loop(0, z_mid, functools.partial(z_body, 0), 0)

    hg[1].forward(rows // 4, rows)

    @pl.when(is_end)
    def _():
        lax.fori_loop(0, kept, functools.partial(h_send, 1), 0)

    @pl.when(is_inner)
    def _():
        lax.fori_loop(z_mid, z_end, functools.partial(z_body, 0), 0)
        lax.fori_loop(0, z_end, functools.partial(z_body, 1), 0)

    for c in range(2):
        cols = slice(c * half, (c + 1) * half)

        def own_first(k, carry):
            out[k, :, cols] = partial(d * share + k, c)
            return carry

        def own_end(k, carry):
            s = d * share + k
            h_feat(c * slots + s).wait_recv()
            out[k, :, cols] += partial_end(s, c)
            return carry

        def own_up(k, carry):
            at = c * slots + d * share + k
            up_copy(at).wait_recv()
            out[k, :, cols] += recv_up[at].astype(F32)
            return carry

        def own_dn(k, carry):
            at = c * slots + d * share + k
            dn_copy(at).wait_recv()
            out[k, :, cols] += recv_dn[at].astype(F32)
            return carry

        lax.fori_loop(0, share, own_first, 0)

        @pl.when(is_next)
        def _():
            lax.fori_loop(0, share, own_end, 0)

        @pl.when(d >= 2)
        def _():
            lax.fori_loop(0, share, own_up, 0)

        @pl.when(d <= last_d - 2)
        def _():
            lax.fori_loop(0, share, own_dn, 0)

    result = pltpu.make_async_copy(out, out_hbm.at[0], local_sem.at[2 * tiles + 4])
    result.start()
    xg.drain()
    hg[0].drain()
    hg[1].drain()
    for t in range(1, rows):
        g_copy(t).wait_send()

    @pl.when(is_end)
    def _():
        dy_feat().wait_send()
        x_feat().wait_send()
        g_feat().wait_send()

        def h_drain(n, carry):
            h_feat(low + n).wait_send()
            h_feat(slots + low + n).wait_send()
            return carry

        lax.fori_loop(0, kept, h_drain, 0)

    def z_drain(s, carry):
        t = s // share

        @pl.when(is_inner & (t > d))
        def _():
            up_copy(s).wait_send()
            up_copy(slots + s).wait_send()

        @pl.when(is_inner & (t < d))
        def _():
            dn_copy(s).wait_send()
            dn_copy(slots + s).wait_send()

        return carry

    lax.fori_loop(0, slots, z_drain, 0)
    result.wait()


def body(rows, depth, node_feat, grad_out, adjacency, tile_count, tile_row, tile_col):
    slots, tile = adjacency.shape[:2]
    feat = node_feat.shape[0]
    tiles = node_feat.shape[1] // tile
    share = slots // depth
    dma = pltpu.SemaphoreType.DMA
    hbm = pl.BlockSpec(memory_space=pltpu.HBM)
    ntiles = rows * tiles
    turned = pltpu.VMEM((tiles, tile, feat), BF16)
    picked = pltpu.VMEM((slots, feat, tile), BF16)
    picked_half = pltpu.VMEM((2 * slots, feat, tile // 2), BF16)
    sums = pltpu.VMEM((2 * slots, tile, tile // 2), BF16)
    return pl.pallas_call(
        functools.partial(kernel, rows, depth),
        out_shape=jax.ShapeDtypeStruct((1, share, tile, tile), F32),
        in_specs=[hbm] * 6,
        out_specs=hbm,
        scratch_shapes=[
            pltpu.VMEM((share, tile, tile), F32),
            pltpu.SMEM(tile_count.shape, jnp.int32),
            pltpu.SMEM(tile_row.shape, jnp.int32),
            pltpu.SMEM(tile_col.shape, jnp.int32),
            pltpu.SMEM((rows * tiles,), jnp.int32),
            pltpu.VMEM((ntiles, feat, tile), BF16),
            pltpu.VMEM((ntiles, feat, tile // 2), BF16),
            pltpu.VMEM((ntiles, feat, tile // 2), BF16),
            pltpu.VMEM((slots, tile, tile), BF16),
            pltpu.VMEM((tiles, feat, tile), BF16),
            turned,
            turned,
            turned,
            turned,
            picked,
            picked_half,
            picked,
            picked_half,
            pltpu.VMEM((slots, feat, tile), F32),
            picked,
            pltpu.VMEM((rows, 2, feat, tile), BF16),
            pltpu.VMEM((rows, 3, feat, tile), BF16),
            pltpu.VMEM((tiles, feat, tile), F32),
            sums,
            sums,
            sums,
            sums,
            dma((2 * tiles + 5,)),
            dma((2 * rows,)),
            dma((2 * rows,)),
            dma((2, 2 * rows)),
            dma((2, 2 * rows)),
            dma((rows,)),
            dma((rows,)),
            dma((2 * slots,)),
            dma((2 * slots,)),
            dma((2 * slots,)),
            dma((2 * slots,)),
            dma((3,)),
            dma((3,)),
            dma((2 * slots,)),
            dma((2 * slots,)),
        ],
        compiler_params=pltpu.CompilerParams(
            collective_id=0, has_side_effects=True, vmem_limit_bytes=62 * 1024 * 1024 + 960 * 1024
        ),
    )(node_feat, grad_out, adjacency, tile_count, tile_row, tile_col)


def solution(mesh):
    in_specs = (P("depth", "rows"), P("depth", "rows"), P("rows", None, None), P(), P(), P())
    out_specs = P("rows", "depth", None, None)
    call = functools.partial(body, mesh.shape["rows"], mesh.shape["depth"])
    return jax.shard_map(call, mesh=mesh, in_specs=in_specs, out_specs=out_specs, check_vma=False)
```

```python
import functools

import jax
import jax.numpy as jnp
from jax import lax
from jax.experimental import pallas as pl
from jax.experimental.pallas import tpu as pltpu
from jax.sharding import PartitionSpec as P

PIECES = 1

MESH = pl.DeviceIdType.MESH
F32 = jnp.float32
BF16 = jnp.bfloat16


def flip(index, mask):
    bit = 1
    out = index
    while bit <= mask:
        if mask & bit:
            out = out + bit * (1 - 2 * ((index // bit) % 2))
        bit *= 2
    return out


def bit_orders(rows):
    bits = []
    bit = 1
    while bit < rows:
        bits.append(bit)
        bit *= 2
    core, chip = bits[:1], bits[1:]
    half = len(chip) // 2
    x_bits, y_bits = chip[:half], chip[half:]
    return (y_bits + x_bits + core, x_bits + y_bits + core)


def peer(index, mask, bits):
    out = index
    for bit in bits:
        out = out + bit * (1 - 2 * ((index // bit) % 2)) * ((mask // bit) % 2)
    return out


class Gather:
    def __init__(self, rows, tiles, buf, send_sem, recv_sem, depth_id, me):
        self.rows, self.tiles, self.buf = rows, tiles, buf
        self.send_sem, self.recv_sem = send_sem, recv_sem
        self.depth_id, self.me = depth_id, me
        self.orders = bit_orders(rows)

    def mask(self, half, place):
        out = 0
        for n, bit in enumerate(self.orders[half]):
            if place >> n & 1:
                out |= bit
        return out

    def copy(self, half, place, n):
        mask = self.mask(half, place)
        bit = self.orders[half][n]
        part = self.tiles // 2
        block = flip(self.me, mask)
        ref = self.buf.at[pl.ds(block * self.tiles + half * part, part)]
        sem = half * self.rows + (mask | bit)
        return pltpu.make_async_remote_copy(
            src_ref=ref,
            dst_ref=ref,
            send_sem=self.send_sem.at[sem],
            recv_sem=self.recv_sem.at[sem],
            device_id=(self.depth_id, flip(self.me, bit)),
            device_id_type=MESH,
        )

    def incoming(self, half, place):
        mask = self.mask(half, place)
        part = self.tiles // 2
        ref = self.buf.at[pl.ds(flip(self.me, mask) * self.tiles + half * part, part)]
        sem = half * self.rows + mask
        return pltpu.make_async_remote_copy(
            src_ref=ref,
            dst_ref=ref,
            send_sem=self.send_sem.at[sem],
            recv_sem=self.recv_sem.at[sem],
            device_id=(self.depth_id, flip(self.me, mask)),
            device_id_type=MESH,
        )

    def start(self):
        for n in range(len(self.orders[0])):
            for half in range(2):
                self.copy(half, 0, n).start()

    def forward(self, begin, end):
        count = len(self.orders[0])
        for place in range(begin, end):
            for half in range(2):
                self.incoming(half, place).wait_recv()
                for n in range(place.bit_length(), count):
                    self.copy(half, place, n).start()

    def drain(self):
        count = len(self.orders[0])
        for place in range(self.rows // 2):
            for half in range(2):
                for n in range(place.bit_length(), count):
                    self.copy(half, place, n).wait_send()


def kernel(
    rows,
    depth,
    x_hbm,
    dy_hbm,
    adj_hbm,
    cnt_hbm,
    trow_hbm,
    tcol_hbm,
    out_hbm,
    out,
    cnt,
    trow,
    tcol,
    gtab,
    xbuf,
    hbuf,
    adj,
    dyt,
    dy_t,
    g_t,
    dy_t2,
    g_t2,
    xpick,
    hpick,
    x2,
    h2,
    terms,
    gterm,
    gout,
    gin,
    gacc,
    send_up,
    send_dn,
    recv_up,
    recv_dn,
    local_sem,
    xs_sem,
    xr_sem,
    hs_sem,
    hr_sem,
    gs_sem,
    gr_sem,
    us_sem,
    ur_sem,
    ds_sem,
    dr_sem,
    feat_ssem,
    feat_rsem,
    h2s_sem,
    h2r_sem,
):
    d = lax.axis_index("depth")
    me = lax.axis_index("rows")
    feat = xbuf.shape[1]
    tile = xbuf.shape[2]
    tiles = dyt.shape[0]
    slots = adj.shape[0]
    share = slots // depth
    last_d = depth - 1
    group = 4
    bits = sorted(bit_orders(rows)[0])

    x_local, dy_local = [], []
    for j in range(tiles):
        cols = pl.ds(j * tile, tile)
        x_local.append(
            pltpu.make_async_copy(x_hbm.at[:, cols], xbuf.at[me * tiles + j], local_sem.at[j])
        )
        dy_local.append(
            pltpu.make_async_copy(dy_hbm.at[:, cols], dyt.at[j], local_sem.at[tiles + j])
        )
    adj_local = pltpu.make_async_copy(adj_hbm, adj, local_sem.at[2 * tiles])
    table_local = [
        pltpu.make_async_copy(src, dst, local_sem.at[2 * tiles + 1 + n])
        for n, (src, dst) in enumerate(((cnt_hbm, cnt), (trow_hbm, trow), (tcol_hbm, tcol)))
    ]
    for c in x_local + table_local + dy_local + [adj_local]:
        c.start()

    barrier = pltpu.get_barrier_semaphore()
    for t in range(1, rows):
        pl.semaphore_signal(
            barrier, inc=1, device_id=(d, (me + t) % rows), device_id_type=MESH
        )
    for t in range(1, depth):
        pl.semaphore_signal(
            barrier, inc=1, device_id=((d + t) % depth, me), device_id_type=MESH
        )

    for c in range(PIECES):
        at = pl.ds(c * slots + d * share, share)

        @pl.when(d <= 1)
        def _():
            recv_up[at] = jnp.zeros((share,) + recv_up.shape[1:], BF16)

        @pl.when(d >= last_d - 1)
        def _():
            recv_dn[at] = jnp.zeros((share,) + recv_dn.shape[1:], BF16)

    for t in range(rows):
        gin[t, 2] = jnp.zeros((feat, tile), BF16)
    gacc[...] = jnp.zeros_like(gacc)

    pl.semaphore_wait(barrier, rows - 1 + depth - 1)

    for c in x_local:
        c.wait()
    xg = Gather(rows, tiles, xbuf, xs_sem, xr_sem, d, me)
    hg = [
        Gather(rows, tiles, hbuf[c], hs_sem.at[c], hr_sem.at[c], d, me) for c in range(PIECES)
    ]
    half = tile // PIECES
    xg.start()
    for c in table_local + dy_local + [adj_local]:
        c.wait()

    my_count = cnt[me]

    def g_body(n, carry):
        for u in range(group):
            s = n * group + u
            g = jnp.dot(dyt[trow[me, s]], adj[s], preferred_element_type=F32)
            gterm[s] = g.astype(BF16)
        return carry

    lax.fori_loop(0, slots // group, g_body, 0)

    def g_pick(t, carry):
        o = peer(me, t, bits)
        first = jnp.int32(0)
        last = jnp.int32(0)
        seen = jnp.int32(0)
        for s in range(slots):
            hit = (s < my_count) & (lax.div(tcol[me, s], jnp.int32(tiles)) == o)
            last = jnp.where(hit, s, last)
            first = jnp.where(hit & (seen == 0), s, first)
            seen = jnp.where(hit, 1, seen)
        gout[t, 0] = gterm[first]
        gout[t, 1] = gterm[last]
        return carry

    lax.fori_loop(0, rows, g_pick, 0)

    def g_copy(t):
        return pltpu.make_async_remote_copy(
            src_ref=gout.at[t],
            dst_ref=gin.at[t, pl.ds(0, 2)],
            send_sem=gs_sem.at[t],
            recv_sem=gr_sem.at[t],
            device_id=(d, flip(me, t)),
            device_id_type=MESH,
        )

    xg.forward(1, rows // 4)
    order = sorted(range(1, rows), key=lambda t: (-bin(t // 2).count("1"), t % 2, t))
    for t in order:
        g_copy(t).start()
    gin[0, pl.ds(0, 2)] = gout[0]

    is_end = (d == 0) | (d == last_d)
    is_next = (d == 1) | (d == last_d - 1)
    inner = jnp.where(d < 2, 1 - d, 2 * last_d - 1 - d)
    inner = jnp.where(d < 2, inner, jnp.where(d >= last_d - 1, inner, 0))
    end_id = (inner, me)
    kept = (depth - 1) * share
    low = jnp.where(d < 2, share, 0)

    def feat_copy(src, dst, n):
        return pltpu.make_async_remote_copy(
            src_ref=src,
            dst_ref=dst,
            send_sem=feat_ssem.at[n],
            recv_sem=feat_rsem.at[n],
            device_id=end_id,
            device_id_type=MESH,
        )

    def dy_feat():
        return feat_copy(dy_t, dy_t2, 0)

    def x_feat():
        at = pl.ds(low, kept)
        return feat_copy(xpick.at[at], x2.at[at], 1)

    def g_feat():
        return feat_copy(g_t, g_t2, 2)

    def h_feat(s):
        return pltpu.make_async_remote_copy(
            src_ref=hpick.at[s],
            dst_ref=h2.at[s],
            send_sem=h2s_sem.at[s],
            recv_sem=h2r_sem.at[s],
            device_id=end_id,
            device_id_type=MESH,
        )

    for j in range(tiles):
        dy_t[j] = dyt[j].astype(F32).T.astype(BF16)

    @pl.when(is_end)
    def _():
        dy_feat().start()

    def g_table(t, carry):
        p = peer(me, t, bits)
        count = cnt[p]
        seen = jnp.int32(0)
        rank = [jnp.int32(2) for _ in range(tiles)]
        for s in range(slots):
            off = tcol[p, s] - me * tiles
            off = jnp.where(s < count, off, -1)
            for j in range(tiles):
                rank[j] = jnp.where(off == j, seen, rank[j])
            seen = jnp.where((off >= 0) & (off < tiles), 1, seen)
        for j in range(tiles):
            gtab[t * tiles + j] = rank[j]
        return carry

    lax.fori_loop(0, rows, g_table, 0)

    xg.forward(rows // 4, rows)

    def h_body(n, carry):
        for u in range(group):
            s = n * group + u
            x = xbuf[tcol[me, s]]
            xpick[s] = x
            terms[s] = lax.dot_general(
                x, adj[s], (((1,), (1,)), ((), ())), preferred_element_type=F32
            )
        return carry

    lax.fori_loop(0, slots // group, h_body, 0)

    @pl.when(is_end)
    def _():
        x_feat().start()

    chunk = min(32, feat)

    def h_sum(c, n, carry):
        at = pl.ds(pl.multiple_of(n * chunk, chunk), chunk)
        total = [jnp.zeros((chunk, half), F32) for _ in range(tiles)]
        for s in range(slots):
            term = terms[s, at, c * half : (c + 1) * half]
            row = jnp.where(s < my_count, trow[me, s], -1)
            for i in range(tiles):
                total[i] = total[i] + jnp.where(row == i, term, 0.0)
        for i in range(tiles):
            hbuf[c][me * tiles + i, at, :] = total[i].astype(BF16)
        return carry

    for c in range(PIECES):
        lax.fori_loop(0, feat // chunk, functools.partial(h_sum, c), 0)
        hg[c].start()
        hg[c].forward(1, rows // 4)

    for t in range(1, rows):
        g_copy(t).wait_recv()

    def g_sum(t, carry):
        for j in range(tiles):
            gacc[j] += gin[t, gtab[t * tiles + j]].astype(F32)
        return carry

    lax.fori_loop(0, rows, g_sum, 0)
    for j in range(tiles):
        g_t[j] = gacc[j].astype(BF16).astype(F32).T.astype(BF16)

    @pl.when(is_end)
    def _():
        g_feat().start()

    hg[0].forward(rows // 4, rows)

    def up_slot(n):
        return (last_d - n // share) * share + n % share

    def h_send(c, n, carry):
        s = jnp.where(d == 0, up_slot(n), n)
        hpick[c * slots + s] = hbuf[c][tcol[me, s]]
        h_feat(c * slots + s).start()
        return carry

    @pl.when(is_end)
    def _():
        lax.fori_loop(0, kept, functools.partial(h_send, 0), 0)

    @pl.when(is_next)
    def _():
        dy_feat().wait_recv()
        x_feat().wait_recv()
        g_feat().wait_recv()

    def partial(s, c, with_end=False):
        row = trow[me, s]
        col = tcol[me, s]
        cols = slice(c * half, (c + 1) * half)
        lhs = [dy_t[row], g_t[row]]
        rhs = [hbuf[c][col], xbuf[col, :, cols]]
        if with_end:
            lhs += [dy_t2[row], g_t2[row]]
            rhs += [h2[c * slots + s], x2[s, :, cols]]
        return jnp.dot(
            jnp.concatenate(lhs, axis=1),
            jnp.concatenate(rhs, axis=0),
            preferred_element_type=F32,
        )

    def up_copy(s):
        return pltpu.make_async_remote_copy(
            src_ref=send_up.at[s],
            dst_ref=recv_up.at[s],
            send_sem=us_sem.at[s],
            recv_sem=ur_sem.at[s],
            device_id=((d + 1) % depth, me),
            device_id_type=MESH,
        )

    def dn_copy(s):
        return pltpu.make_async_remote_copy(
            src_ref=send_dn.at[s],
            dst_ref=recv_dn.at[s],
            send_sem=ds_sem.at[s],
            recv_sem=dr_sem.at[s],
            device_id=((d + depth - 1) % depth, me),
            device_id_type=MESH,
        )

    def up_step(n, c):
        s = up_slot(n)
        at = c * slots + s

        @pl.when((d == 1) & (n < (last_d - 1) * share))
        def _():
            h_feat(at).wait_recv()
            send_up[at] = partial(s, c, True).astype(BF16)
            up_copy(at).start()

        @pl.when((d > 1) & (d < last_d) & (n < (last_d - d) * share))
        def _():
            p = partial(s, c)
            up_copy(at).wait_recv()
            send_up[at] = (p + recv_up[at].astype(F32)).astype(BF16)
            up_copy(at).start()

    def dn_step(n, c):
        at = c * slots + n

        @pl.when((d == last_d - 1) & (n < d * share))
        def _():
            h_feat(at).wait_recv()
            send_dn[at] = partial(n, c, True).astype(BF16)
            dn_copy(at).start()

        @pl.when((d > 0) & (d < last_d - 1) & (n < d * share))
        def _():
            p = partial(n, c)
            dn_copy(at).wait_recv()
            send_dn[at] = (p + recv_dn[at].astype(F32)).astype(BF16)
            dn_copy(at).start()

    lag = 1

    z_end = (last_d - 1) * share + lag
    is_inner = (d > 0) & (d < last_d)

    def own_step(k, c):
        s = d * share + k
        cols = slice(c * half, (c + 1) * half)

        @pl.when(is_next)
        def _():
            h_feat(c * slots + s).wait_recv()
            out[k, :, cols] = partial(s, c, True)

        @pl.when((d != 1) & (d != last_d - 1))
        def _():
            out[k, :, cols] = partial(s, c)

    def z_body(c, n, carry):
        @pl.when(d < last_d - 1)
        def _():
            up_step(n, c)

            @pl.when(n >= lag)
            def _():
                dn_step(n - lag, c)

        @pl.when(d == last_d - 1)
        def _():
            dn_step(n, c)

            @pl.when(n >= lag)
            def _():
                up_step(n - lag, c)

        @pl.when(n >= z_end - share)
        def _():
            own_step(n - (z_end - share), c)

        return carry

    def z_range(c, begin, end):
        @pl.when(is_inner)
        def _():
            lax.fori_loop(begin, end, functools.partial(z_body, c), 0)

    def own_range(c):
        @pl.when(is_end)
        def _():
            lax.fori_loop(0, share, lambda k, carry: (own_step(k, c), carry)[1], 0)

    for c in range(PIECES):
        z_mid = z_end // 2 if c + 1 < PIECES else z_end
        z_range(c, 0, z_mid)
        own_range(c)
        if c + 1 < PIECES:
            hg[c + 1].forward(rows // 4, rows)

            @pl.when(is_end)
            def _():
                lax.fori_loop(0, kept, functools.partial(h_send, c + 1), 0)

        z_range(c, z_mid, z_end)

    def result_copy(k):
        return pltpu.make_async_copy(
            out.at[k], out_hbm.at[0, k], local_sem.at[2 * tiles + 4 + k]
        )

    def finish(k, carry):
        s = d * share + k
        for c in range(PIECES):
            at = c * slots + s
            cols = slice(c * half, (c + 1) * half)

            @pl.when(d >= 2)
            def _():
                up_copy(at).wait_recv()

            @pl.when(d <= last_d - 2)
            def _():
                dn_copy(at).wait_recv()

            total = out[k, :, cols] + recv_up[at].astype(F32) + recv_dn[at].astype(F32)
            out[k, :, cols] = jnp.where(s < my_count, total, 0.0)
        result_copy(k).start()
        return carry

    lax.fori_loop(0, share, finish, 0)

    xg.drain()
    for c in range(PIECES):
        hg[c].drain()
    for t in range(1, rows):
        g_copy(t).wait_send()

    @pl.when(is_end)
    def _():
        dy_feat().wait_send()
        x_feat().wait_send()
        g_feat().wait_send()

        def h_drain(n, carry):
            for c in range(PIECES):
                h_feat(c * slots + low + n).wait_send()
            return carry

        lax.fori_loop(0, kept, h_drain, 0)

    def z_drain(s, carry):
        t = s // share

        @pl.when(is_inner & (t > d))
        def _():
            for c in range(PIECES):
                up_copy(c * slots + s).wait_send()

        @pl.when(is_inner & (t < d))
        def _():
            for c in range(PIECES):
                dn_copy(c * slots + s).wait_send()

        return carry

    lax.fori_loop(0, slots, z_drain, 0)
    for k in range(share):
        result_copy(k).wait()


def body(rows, depth, node_feat, grad_out, adjacency, tile_count, tile_row, tile_col):
    slots, tile = adjacency.shape[:2]
    feat = node_feat.shape[0]
    tiles = node_feat.shape[1] // tile
    share = slots // depth
    dma = pltpu.SemaphoreType.DMA
    hbm = pl.BlockSpec(memory_space=pltpu.HBM)
    ntiles = rows * tiles
    turned = pltpu.VMEM((tiles, tile, feat), BF16)
    picked = pltpu.VMEM((slots, feat, tile), BF16)
    picked_half = pltpu.VMEM((PIECES * slots, feat, tile // PIECES), BF16)
    sums = pltpu.VMEM((PIECES * slots, tile, tile // PIECES), BF16)
    return pl.pallas_call(
        functools.partial(kernel, rows, depth),
        out_shape=jax.ShapeDtypeStruct((1, share, tile, tile), F32),
        in_specs=[hbm] * 6,
        out_specs=hbm,
        scratch_shapes=[
            pltpu.VMEM((share, tile, tile), F32),
            pltpu.SMEM(tile_count.shape, jnp.int32),
            pltpu.SMEM(tile_row.shape, jnp.int32),
            pltpu.SMEM(tile_col.shape, jnp.int32),
            pltpu.SMEM((rows * tiles,), jnp.int32),
            pltpu.VMEM((ntiles, feat, tile), BF16),
            [pltpu.VMEM((ntiles, feat, tile // PIECES), BF16)] * PIECES,
            pltpu.VMEM((slots, tile, tile), BF16),
            pltpu.VMEM((tiles, feat, tile), BF16),
            turned,
            turned,
            turned,
            turned,
            picked,
            picked_half,
            picked,
            picked_half,
            pltpu.VMEM((slots, feat, tile), F32),
            picked,
            pltpu.VMEM((rows, 2, feat, tile), BF16),
            pltpu.VMEM((rows, 3, feat, tile), BF16),
            pltpu.VMEM((tiles, feat, tile), F32),
            sums,
            sums,
            sums,
            sums,
            dma((2 * tiles + 4 + share,)),
            dma((2 * rows,)),
            dma((2 * rows,)),
            dma((PIECES, 2 * rows)),
            dma((PIECES, 2 * rows)),
            dma((rows,)),
            dma((rows,)),
            dma((PIECES * slots,)),
            dma((PIECES * slots,)),
            dma((PIECES * slots,)),
            dma((PIECES * slots,)),
            dma((3,)),
            dma((3,)),
            dma((PIECES * slots,)),
            dma((PIECES * slots,)),
        ],
        compiler_params=pltpu.CompilerParams(
            collective_id=0, has_side_effects=True, vmem_limit_bytes=64 * 1024 * 1024
        ),
    )(node_feat, grad_out, adjacency, tile_count, tile_row, tile_col)


def solution(mesh):
    in_specs = (P("depth", "rows"), P("depth", "rows"), P("rows", None, None), P(), P(), P())
    out_specs = P("rows", "depth", None, None)
    call = functools.partial(body, mesh.shape["rows"], mesh.shape["depth"])
    return jax.shard_map(call, mesh=mesh, in_specs=in_specs, out_specs=out_specs, check_vma=False)
```

```python
import functools

import jax
import jax.numpy as jnp
from jax import lax
from jax.experimental import pallas as pl
from jax.experimental.pallas import tpu as pltpu
from jax.sharding import PartitionSpec as P

PIECES = 2

MESH = pl.DeviceIdType.MESH
F32 = jnp.float32
BF16 = jnp.bfloat16


def flip(index, mask):
    bit = 1
    out = index
    while bit <= mask:
        if mask & bit:
            out = out + bit * (1 - 2 * ((index // bit) % 2))
        bit *= 2
    return out


def bit_orders(rows):
    bits = []
    bit = 1
    while bit < rows:
        bits.append(bit)
        bit *= 2
    core, chip = bits[:1], bits[1:]
    half = len(chip) // 2
    x_bits, y_bits = chip[:half], chip[half:]
    return (y_bits + x_bits + core, x_bits + y_bits + core)


def peer(index, mask, bits):
    out = index
    for bit in bits:
        out = out + bit * (1 - 2 * ((index // bit) % 2)) * ((mask // bit) % 2)
    return out


class Gather:
    def __init__(self, rows, tiles, buf, send_sem, recv_sem, depth_id, me):
        self.rows, self.tiles, self.buf = rows, tiles, buf
        self.send_sem, self.recv_sem = send_sem, recv_sem
        self.depth_id, self.me = depth_id, me
        self.orders = bit_orders(rows)

    def mask(self, half, place):
        out = 0
        for n, bit in enumerate(self.orders[half]):
            if place >> n & 1:
                out |= bit
        return out

    def copy(self, half, place, n):
        mask = self.mask(half, place)
        bit = self.orders[half][n]
        part = self.tiles // 2
        block = flip(self.me, mask)
        ref = self.buf.at[pl.ds(block * self.tiles + half * part, part)]
        sem = half * self.rows + (mask | bit)
        return pltpu.make_async_remote_copy(
            src_ref=ref,
            dst_ref=ref,
            send_sem=self.send_sem.at[sem],
            recv_sem=self.recv_sem.at[sem],
            device_id=(self.depth_id, flip(self.me, bit)),
            device_id_type=MESH,
        )

    def incoming(self, half, place):
        mask = self.mask(half, place)
        part = self.tiles // 2
        ref = self.buf.at[pl.ds(flip(self.me, mask) * self.tiles + half * part, part)]
        sem = half * self.rows + mask
        return pltpu.make_async_remote_copy(
            src_ref=ref,
            dst_ref=ref,
            send_sem=self.send_sem.at[sem],
            recv_sem=self.recv_sem.at[sem],
            device_id=(self.depth_id, flip(self.me, mask)),
            device_id_type=MESH,
        )

    def start(self):
        for n in range(len(self.orders[0])):
            for half in range(2):
                self.copy(half, 0, n).start()

    def forward(self, begin, end):
        count = len(self.orders[0])
        for place in range(begin, end):
            for half in range(2):
                self.incoming(half, place).wait_recv()
                for n in range(place.bit_length(), count):
                    self.copy(half, place, n).start()

    def drain(self):
        count = len(self.orders[0])
        for place in range(self.rows // 2):
            for half in range(2):
                for n in range(place.bit_length(), count):
                    self.copy(half, place, n).wait_send()


def kernel(
    rows,
    depth,
    x_hbm,
    dy_hbm,
    adj_hbm,
    cnt_hbm,
    trow_hbm,
    tcol_hbm,
    out_hbm,
    out,
    cnt,
    trow,
    tcol,
    gtab,
    xbuf,
    hbuf,
    adj,
    dyt,
    dy_t,
    g_t,
    dy_t2,
    g_t2,
    xpick,
    hpick,
    x2,
    h2,
    terms,
    gterm,
    gout,
    gin,
    gacc,
    send_up,
    send_dn,
    recv_up,
    recv_dn,
    local_sem,
    xs_sem,
    xr_sem,
    hs_sem,
    hr_sem,
    gs_sem,
    gr_sem,
    us_sem,
    ur_sem,
    ds_sem,
    dr_sem,
    feat_ssem,
    feat_rsem,
    h2s_sem,
    h2r_sem,
):
    d = lax.axis_index("depth")
    me = lax.axis_index("rows")
    feat = xbuf.shape[1]
    tile = xbuf.shape[2]
    tiles = dyt.shape[0]
    slots = adj.shape[0]
    share = slots // depth
    last_d = depth - 1
    group = 4
    bits = sorted(bit_orders(rows)[0])

    x_local, dy_local = [], []
    for j in range(tiles):
        cols = pl.ds(j * tile, tile)
        x_local.append(
            pltpu.make_async_copy(x_hbm.at[:, cols], xbuf.at[me * tiles + j], local_sem.at[j])
        )
        dy_local.append(
            pltpu.make_async_copy(dy_hbm.at[:, cols], dyt.at[j], local_sem.at[tiles + j])
        )
    adj_local = pltpu.make_async_copy(adj_hbm, adj, local_sem.at[2 * tiles])
    table_local = [
        pltpu.make_async_copy(src, dst, local_sem.at[2 * tiles + 1 + n])
        for n, (src, dst) in enumerate(((cnt_hbm, cnt), (trow_hbm, trow), (tcol_hbm, tcol)))
    ]
    for c in x_local + table_local + dy_local + [adj_local]:
        c.start()

    barrier = pltpu.get_barrier_semaphore()
    for t in range(1, rows):
        pl.semaphore_signal(
            barrier, inc=1, device_id=(d, (me + t) % rows), device_id_type=MESH
        )
    for t in range(1, depth):
        pl.semaphore_signal(
            barrier, inc=1, device_id=((d + t) % depth, me), device_id_type=MESH
        )

    for c in range(PIECES):
        at = pl.ds(c * slots + d * share, share)

        @pl.when(d <= 1)
        def _():
            recv_up[at] = jnp.zeros((share,) + recv_up.shape[1:], BF16)

        @pl.when(d >= last_d - 1)
        def _():
            recv_dn[at] = jnp.zeros((share,) + recv_dn.shape[1:], BF16)

    for t in range(rows):
        gin[t, 2] = jnp.zeros((feat, tile), BF16)
    gacc[...] = jnp.zeros_like(gacc)

    pl.semaphore_wait(barrier, rows - 1 + depth - 1)

    for c in x_local:
        c.wait()
    xg = Gather(rows, tiles, xbuf, xs_sem, xr_sem, d, me)
    hg = [
        Gather(rows, tiles, hbuf[c], hs_sem.at[c], hr_sem.at[c], d, me) for c in range(PIECES)
    ]
    half = tile // PIECES
    xg.start()
    for c in table_local + dy_local + [adj_local]:
        c.wait()

    my_count = cnt[me]

    def g_body(n, carry):
        for u in range(group):
            s = n * group + u
            g = jnp.dot(dyt[trow[me, s]], adj[s], preferred_element_type=F32)
            gterm[s] = g.astype(BF16)
        return carry

    lax.fori_loop(0, slots // group, g_body, 0)

    def g_pick(t, carry):
        o = peer(me, t, bits)
        first = jnp.int32(0)
        last = jnp.int32(0)
        seen = jnp.int32(0)
        for s in range(slots):
            hit = (s < my_count) & (lax.div(tcol[me, s], jnp.int32(tiles)) == o)
            last = jnp.where(hit, s, last)
            first = jnp.where(hit & (seen == 0), s, first)
            seen = jnp.where(hit, 1, seen)
        gout[t, 0] = gterm[first]
        gout[t, 1] = gterm[last]
        return carry

    lax.fori_loop(0, rows, g_pick, 0)

    def g_copy(t):
        return pltpu.make_async_remote_copy(
            src_ref=gout.at[t],
            dst_ref=gin.at[t, pl.ds(0, 2)],
            send_sem=gs_sem.at[t],
            recv_sem=gr_sem.at[t],
            device_id=(d, flip(me, t)),
            device_id_type=MESH,
        )

    xg.forward(1, rows // 4)
    order = sorted(range(1, rows), key=lambda t: (-bin(t // 2).count("1"), t % 2, t))
    for t in order:
        g_copy(t).start()
    gin[0, pl.ds(0, 2)] = gout[0]

    is_end = (d == 0) | (d == last_d)
    is_next = (d == 1) | (d == last_d - 1)
    inner = jnp.where(d < 2, 1 - d, 2 * last_d - 1 - d)
    inner = jnp.where(d < 2, inner, jnp.where(d >= last_d - 1, inner, 0))
    end_id = (inner, me)
    kept = (depth - 1) * share
    low = jnp.where(d < 2, share, 0)

    def feat_copy(src, dst, n):
        return pltpu.make_async_remote_copy(
            src_ref=src,
            dst_ref=dst,
            send_sem=feat_ssem.at[n],
            recv_sem=feat_rsem.at[n],
            device_id=end_id,
            device_id_type=MESH,
        )

    def dy_feat():
        return feat_copy(dy_t, dy_t2, 0)

    def x_feat():
        at = pl.ds(low, kept)
        return feat_copy(xpick.at[at], x2.at[at], 1)

    def g_feat():
        return feat_copy(g_t, g_t2, 2)

    def h_feat(s):
        return pltpu.make_async_remote_copy(
            src_ref=hpick.at[s],
            dst_ref=h2.at[s],
            send_sem=h2s_sem.at[s],
            recv_sem=h2r_sem.at[s],
            device_id=end_id,
            device_id_type=MESH,
        )

    for j in range(tiles):
        dy_t[j] = dyt[j].astype(F32).T.astype(BF16)

    @pl.when(is_end)
    def _():
        dy_feat().start()

    def g_table(t, carry):
        p = peer(me, t, bits)
        count = cnt[p]
        seen = jnp.int32(0)
        rank = [jnp.int32(2) for _ in range(tiles)]
        for s in range(slots):
            off = tcol[p, s] - me * tiles
            off = jnp.where(s < count, off, -1)
            for j in range(tiles):
                rank[j] = jnp.where(off == j, seen, rank[j])
            seen = jnp.where((off >= 0) & (off < tiles), 1, seen)
        for j in range(tiles):
            gtab[t * tiles + j] = rank[j]
        return carry

    lax.fori_loop(0, rows, g_table, 0)

    xg.forward(rows // 4, rows)

    def h_body(n, carry):
        for u in range(group):
            s = n * group + u
            x = xbuf[tcol[me, s]]
            xpick[s] = x
            terms[s] = lax.dot_general(
                x, adj[s], (((1,), (1,)), ((), ())), preferred_element_type=F32
            )
        return carry

    lax.fori_loop(0, slots // group, h_body, 0)

    @pl.when(is_end)
    def _():
        x_feat().start()

    chunk = min(32, feat)

    def h_sum(c, n, carry):
        at = pl.ds(pl.multiple_of(n * chunk, chunk), chunk)
        total = [jnp.zeros((chunk, half), F32) for _ in range(tiles)]
        for s in range(slots):
            term = terms[s, at, c * half : (c + 1) * half]
            row = jnp.where(s < my_count, trow[me, s], -1)
            for i in range(tiles):
                total[i] = total[i] + jnp.where(row == i, term, 0.0)
        for i in range(tiles):
            hbuf[c][me * tiles + i, at, :] = total[i].astype(BF16)
        return carry

    for c in range(PIECES):
        lax.fori_loop(0, feat // chunk, functools.partial(h_sum, c), 0)
        hg[c].start()
        hg[c].forward(1, rows // 4)

    for t in range(1, rows):
        g_copy(t).wait_recv()

    def g_sum(t, carry):
        for j in range(tiles):
            gacc[j] += gin[t, gtab[t * tiles + j]].astype(F32)
        return carry

    lax.fori_loop(0, rows, g_sum, 0)
    for j in range(tiles):
        g_t[j] = gacc[j].astype(BF16).astype(F32).T.astype(BF16)

    @pl.when(is_end)
    def _():
        g_feat().start()

    hg[0].forward(rows // 4, rows)

    def up_slot(n):
        return (last_d - n // share) * share + n % share

    def h_send(c, n, carry):
        s = jnp.where(d == 0, up_slot(n), n)
        hpick[c * slots + s] = hbuf[c][tcol[me, s]]
        h_feat(c * slots + s).start()
        return carry

    @pl.when(is_end)
    def _():
        lax.fori_loop(0, kept, functools.partial(h_send, 0), 0)

    @pl.when(is_next)
    def _():
        dy_feat().wait_recv()
        x_feat().wait_recv()
        g_feat().wait_recv()

    def partial(s, c, with_end=False):
        row = trow[me, s]
        col = tcol[me, s]
        cols = slice(c * half, (c + 1) * half)
        lhs = [dy_t[row], g_t[row]]
        rhs = [hbuf[c][col], xbuf[col, :, cols]]
        if with_end:
            lhs += [dy_t2[row], g_t2[row]]
            rhs += [h2[c * slots + s], x2[s, :, cols]]
        return jnp.dot(
            jnp.concatenate(lhs, axis=1),
            jnp.concatenate(rhs, axis=0),
            preferred_element_type=F32,
        )

    def up_copy(s):
        return pltpu.make_async_remote_copy(
            src_ref=send_up.at[s],
            dst_ref=recv_up.at[s],
            send_sem=us_sem.at[s],
            recv_sem=ur_sem.at[s],
            device_id=((d + 1) % depth, me),
            device_id_type=MESH,
        )

    def dn_copy(s):
        return pltpu.make_async_remote_copy(
            src_ref=send_dn.at[s],
            dst_ref=recv_dn.at[s],
            send_sem=ds_sem.at[s],
            recv_sem=dr_sem.at[s],
            device_id=((d + depth - 1) % depth, me),
            device_id_type=MESH,
        )

    def up_step(n, c):
        s = up_slot(n)
        at = c * slots + s

        @pl.when((d == 1) & (n < (last_d - 1) * share))
        def _():
            h_feat(at).wait_recv()
            send_up[at] = partial(s, c, True).astype(BF16)
            up_copy(at).start()

        @pl.when((d > 1) & (d < last_d) & (n < (last_d - d) * share))
        def _():
            p = partial(s, c)
            up_copy(at).wait_recv()
            send_up[at] = (p + recv_up[at].astype(F32)).astype(BF16)
            up_copy(at).start()

    def dn_step(n, c):
        at = c * slots + n

        @pl.when((d == last_d - 1) & (n < d * share))
        def _():
            h_feat(at).wait_recv()
            send_dn[at] = partial(n, c, True).astype(BF16)
            dn_copy(at).start()

        @pl.when((d > 0) & (d < last_d - 1) & (n < d * share))
        def _():
            p = partial(n, c)
            dn_copy(at).wait_recv()
            send_dn[at] = (p + recv_dn[at].astype(F32)).astype(BF16)
            dn_copy(at).start()

    lag = 1

    z_end = (last_d - 1) * share + lag
    is_inner = (d > 0) & (d < last_d)

    def own_step(k, c):
        s = d * share + k
        cols = slice(c * half, (c + 1) * half)

        @pl.when(is_next)
        def _():
            h_feat(c * slots + s).wait_recv()
            out[k, :, cols] = partial(s, c, True)

        @pl.when((d != 1) & (d != last_d - 1))
        def _():
            out[k, :, cols] = partial(s, c)

    def z_body(c, n, carry):
        @pl.when(d < last_d - 1)
        def _():
            up_step(n, c)

            @pl.when(n >= lag)
            def _():
                dn_step(n - lag, c)

        @pl.when(d == last_d - 1)
        def _():
            dn_step(n, c)

            @pl.when(n >= lag)
            def _():
                up_step(n - lag, c)

        @pl.when(n >= z_end - share)
        def _():
            own_step(n - (z_end - share), c)

        return carry

    def z_range(c, begin, end):
        @pl.when(is_inner)
        def _():
            lax.fori_loop(begin, end, functools.partial(z_body, c), 0)

    def own_range(c):
        @pl.when(is_end)
        def _():
            lax.fori_loop(0, share, lambda k, carry: (own_step(k, c), carry)[1], 0)

    for c in range(PIECES):
        z_mid = z_end // 2 if c + 1 < PIECES else z_end
        z_range(c, 0, z_mid)
        own_range(c)
        if c + 1 < PIECES:
            hg[c + 1].forward(rows // 4, rows)

            @pl.when(is_end)
            def _():
                lax.fori_loop(0, kept, functools.partial(h_send, c + 1), 0)

        z_range(c, z_mid, z_end)

    def result_copy(k):
        return pltpu.make_async_copy(
            out.at[k], out_hbm.at[0, k], local_sem.at[2 * tiles + 4 + k]
        )

    def finish(k, carry):
        s = d * share + k
        for c in range(PIECES):
            at = c * slots + s
            cols = slice(c * half, (c + 1) * half)

            @pl.when(d >= 2)
            def _():
                up_copy(at).wait_recv()

            @pl.when(d <= last_d - 2)
            def _():
                dn_copy(at).wait_recv()

            total = out[k, :, cols] + recv_up[at].astype(F32) + recv_dn[at].astype(F32)
            out[k, :, cols] = jnp.where(s < my_count, total, 0.0)
        result_copy(k).start()
        return carry

    lax.fori_loop(0, share, finish, 0)

    xg.drain()
    for c in range(PIECES):
        hg[c].drain()
    for t in range(1, rows):
        g_copy(t).wait_send()

    @pl.when(is_end)
    def _():
        dy_feat().wait_send()
        x_feat().wait_send()
        g_feat().wait_send()

        def h_drain(n, carry):
            for c in range(PIECES):
                h_feat(c * slots + low + n).wait_send()
            return carry

        lax.fori_loop(0, kept, h_drain, 0)

    def z_drain(s, carry):
        t = s // share

        @pl.when(is_inner & (t > d))
        def _():
            for c in range(PIECES):
                up_copy(c * slots + s).wait_send()

        @pl.when(is_inner & (t < d))
        def _():
            for c in range(PIECES):
                dn_copy(c * slots + s).wait_send()

        return carry

    lax.fori_loop(0, slots, z_drain, 0)
    for k in range(share):
        result_copy(k).wait()


def body(rows, depth, node_feat, grad_out, adjacency, tile_count, tile_row, tile_col):
    slots, tile = adjacency.shape[:2]
    feat = node_feat.shape[0]
    tiles = node_feat.shape[1] // tile
    share = slots // depth
    dma = pltpu.SemaphoreType.DMA
    hbm = pl.BlockSpec(memory_space=pltpu.HBM)
    ntiles = rows * tiles
    turned = pltpu.VMEM((tiles, tile, feat), BF16)
    picked = pltpu.VMEM((slots, feat, tile), BF16)
    picked_half = pltpu.VMEM((PIECES * slots, feat, tile // PIECES), BF16)
    sums = pltpu.VMEM((PIECES * slots, tile, tile // PIECES), BF16)
    return pl.pallas_call(
        functools.partial(kernel, rows, depth),
        out_shape=jax.ShapeDtypeStruct((1, share, tile, tile), F32),
        in_specs=[hbm] * 6,
        out_specs=hbm,
        scratch_shapes=[
            pltpu.VMEM((share, tile, tile), F32),
            pltpu.SMEM(tile_count.shape, jnp.int32),
            pltpu.SMEM(tile_row.shape, jnp.int32),
            pltpu.SMEM(tile_col.shape, jnp.int32),
            pltpu.SMEM((rows * tiles,), jnp.int32),
            pltpu.VMEM((ntiles, feat, tile), BF16),
            [pltpu.VMEM((ntiles, feat, tile // PIECES), BF16)] * PIECES,
            pltpu.VMEM((slots, tile, tile), BF16),
            pltpu.VMEM((tiles, feat, tile), BF16),
            turned,
            turned,
            turned,
            turned,
            picked,
            picked_half,
            picked,
            picked_half,
            pltpu.VMEM((slots, feat, tile), F32),
            picked,
            pltpu.VMEM((rows, 2, feat, tile), BF16),
            pltpu.VMEM((rows, 3, feat, tile), BF16),
            pltpu.VMEM((tiles, feat, tile), F32),
            sums,
            sums,
            sums,
            sums,
            dma((2 * tiles + 4 + share,)),
            dma((2 * rows,)),
            dma((2 * rows,)),
            dma((PIECES, 2 * rows)),
            dma((PIECES, 2 * rows)),
            dma((rows,)),
            dma((rows,)),
            dma((PIECES * slots,)),
            dma((PIECES * slots,)),
            dma((PIECES * slots,)),
            dma((PIECES * slots,)),
            dma((3,)),
            dma((3,)),
            dma((PIECES * slots,)),
            dma((PIECES * slots,)),
        ],
        compiler_params=pltpu.CompilerParams(
            collective_id=0, has_side_effects=True, vmem_limit_bytes=64 * 1024 * 1024
        ),
    )(node_feat, grad_out, adjacency, tile_count, tile_row, tile_col)


def solution(mesh):
    in_specs = (P("depth", "rows"), P("depth", "rows"), P("rows", None, None), P(), P(), P())
    out_specs = P("rows", "depth", None, None)
    call = functools.partial(body, mesh.shape["rows"], mesh.shape["depth"])
    return jax.shard_map(call, mesh=mesh, in_specs=in_specs, out_specs=out_specs, check_vma=False)
```

```python
import functools

import jax
import jax.numpy as jnp
from jax import lax
from jax.experimental import pallas as pl
from jax.experimental.pallas import tpu as pltpu
from jax.sharding import PartitionSpec as P

PIECES = 1
WINDOW = 2

MESH = pl.DeviceIdType.MESH
F32 = jnp.float32
BF16 = jnp.bfloat16


def flip(index, mask):
    bit = 1
    out = index
    while bit <= mask:
        if mask & bit:
            out = out + bit * (1 - 2 * ((index // bit) % 2))
        bit *= 2
    return out


def bit_orders(rows):
    bits = []
    bit = 1
    while bit < rows:
        bits.append(bit)
        bit *= 2
    core, chip = bits[:1], bits[1:]
    half = len(chip) // 2
    x_bits, y_bits = chip[:half], chip[half:]
    return (y_bits + x_bits + core, x_bits + y_bits + core)


def peer(index, mask, bits):
    out = index
    for bit in bits:
        out = out + bit * (1 - 2 * ((index // bit) % 2)) * ((mask // bit) % 2)
    return out


class Gather:
    def __init__(self, rows, tiles, buf, send_sem, recv_sem, depth_id, me):
        self.rows, self.tiles, self.buf = rows, tiles, buf
        self.send_sem, self.recv_sem = send_sem, recv_sem
        self.depth_id, self.me = depth_id, me
        self.orders = bit_orders(rows)

    def mask(self, half, place):
        out = 0
        for n, bit in enumerate(self.orders[half]):
            if place >> n & 1:
                out |= bit
        return out

    def copy(self, half, place, n):
        mask = self.mask(half, place)
        bit = self.orders[half][n]
        part = self.tiles // 2
        block = flip(self.me, mask)
        ref = self.buf.at[pl.ds(block * self.tiles + half * part, part)]
        sem = half * self.rows + (mask | bit)
        return pltpu.make_async_remote_copy(
            src_ref=ref,
            dst_ref=ref,
            send_sem=self.send_sem.at[sem],
            recv_sem=self.recv_sem.at[sem],
            device_id=(self.depth_id, flip(self.me, bit)),
            device_id_type=MESH,
        )

    def incoming(self, half, place):
        mask = self.mask(half, place)
        part = self.tiles // 2
        ref = self.buf.at[pl.ds(flip(self.me, mask) * self.tiles + half * part, part)]
        sem = half * self.rows + mask
        return pltpu.make_async_remote_copy(
            src_ref=ref,
            dst_ref=ref,
            send_sem=self.send_sem.at[sem],
            recv_sem=self.recv_sem.at[sem],
            device_id=(self.depth_id, flip(self.me, mask)),
            device_id_type=MESH,
        )

    def start(self):
        for n in range(len(self.orders[0])):
            for half in range(2):
                self.copy(half, 0, n).start()

    def forward(self, begin, end):
        count = len(self.orders[0])
        for place in range(begin, end):
            for half in range(2):
                self.incoming(half, place).wait_recv()
                for n in range(place.bit_length(), count):
                    self.copy(half, place, n).start()

    def drain(self):
        count = len(self.orders[0])
        for place in range(self.rows // 2):
            for half in range(2):
                for n in range(place.bit_length(), count):
                    self.copy(half, place, n).wait_send()


def kernel(
    rows,
    depth,
    x_hbm,
    dy_hbm,
    adj_hbm,
    cnt_hbm,
    trow_hbm,
    tcol_hbm,
    out_hbm,
    out,
    cnt,
    trow,
    tcol,
    gtab,
    xbuf,
    hbuf,
    adj,
    dyt,
    dy_t,
    g_t,
    dy_t2,
    g_t2,
    xpick,
    hpick,
    x2,
    h2,
    terms,
    gterm,
    gout,
    gin,
    gacc,
    send_up,
    send_dn,
    recv_up,
    recv_dn,
    local_sem,
    xs_sem,
    xr_sem,
    hs_sem,
    hr_sem,
    gs_sem,
    gr_sem,
    us_sem,
    ur_sem,
    ds_sem,
    dr_sem,
    feat_ssem,
    feat_rsem,
    h2s_sem,
    h2r_sem,
):
    d = lax.axis_index("depth")
    me = lax.axis_index("rows")
    feat = xbuf.shape[1]
    tile = xbuf.shape[2]
    tiles = dyt.shape[0]
    slots = adj.shape[0]
    share = slots // depth
    last_d = depth - 1
    group = 4
    bits = sorted(bit_orders(rows)[0])

    x_local, dy_local = [], []
    for j in range(tiles):
        cols = pl.ds(j * tile, tile)
        x_local.append(
            pltpu.make_async_copy(x_hbm.at[:, cols], xbuf.at[me * tiles + j], local_sem.at[j])
        )
        dy_local.append(
            pltpu.make_async_copy(dy_hbm.at[:, cols], dyt.at[j], local_sem.at[tiles + j])
        )
    adj_local = pltpu.make_async_copy(adj_hbm, adj, local_sem.at[2 * tiles])
    table_local = [
        pltpu.make_async_copy(src, dst, local_sem.at[2 * tiles + 1 + n])
        for n, (src, dst) in enumerate(((cnt_hbm, cnt), (trow_hbm, trow), (tcol_hbm, tcol)))
    ]
    for c in x_local + table_local + dy_local + [adj_local]:
        c.start()

    barrier = pltpu.get_barrier_semaphore()
    for t in range(1, rows):
        pl.semaphore_signal(
            barrier, inc=1, device_id=(d, (me + t) % rows), device_id_type=MESH
        )
    for t in range(1, depth):
        pl.semaphore_signal(
            barrier, inc=1, device_id=((d + t) % depth, me), device_id_type=MESH
        )

    for c in range(PIECES):
        at = pl.ds(c * slots + d * share, share)

        @pl.when(d <= 1)
        def _():
            recv_up[at] = jnp.zeros((share,) + recv_up.shape[1:], BF16)

        @pl.when(d >= last_d - 1)
        def _():
            recv_dn[at] = jnp.zeros((share,) + recv_dn.shape[1:], BF16)

    for t in range(rows):
        gin[t, 2] = jnp.zeros((feat, tile), BF16)
    gacc[...] = jnp.zeros_like(gacc)

    pl.semaphore_wait(barrier, rows - 1 + depth - 1)

    for c in x_local:
        c.wait()
    xg = Gather(rows, tiles, xbuf, xs_sem, xr_sem, d, me)
    hg = [
        Gather(rows, tiles, hbuf[c], hs_sem.at[c], hr_sem.at[c], d, me) for c in range(PIECES)
    ]
    half = tile // PIECES
    xg.start()
    for c in table_local + dy_local + [adj_local]:
        c.wait()

    my_count = cnt[me]

    def g_body(n, carry):
        for u in range(group):
            s = n * group + u
            g = jnp.dot(dyt[trow[me, s]], adj[s], preferred_element_type=F32)
            gterm[s] = g.astype(BF16)
        return carry

    lax.fori_loop(0, slots // group, g_body, 0)

    def g_pick(t, carry):
        o = peer(me, t, bits)
        first = jnp.int32(0)
        last = jnp.int32(0)
        seen = jnp.int32(0)
        for s in range(slots):
            hit = (s < my_count) & (lax.div(tcol[me, s], jnp.int32(tiles)) == o)
            last = jnp.where(hit, s, last)
            first = jnp.where(hit & (seen == 0), s, first)
            seen = jnp.where(hit, 1, seen)
        gout[t, 0] = gterm[first]
        gout[t, 1] = gterm[last]
        return carry

    lax.fori_loop(0, rows, g_pick, 0)

    def g_copy(t):
        return pltpu.make_async_remote_copy(
            src_ref=gout.at[t],
            dst_ref=gin.at[t, pl.ds(0, 2)],
            send_sem=gs_sem.at[t],
            recv_sem=gr_sem.at[t],
            device_id=(d, flip(me, t)),
            device_id_type=MESH,
        )

    xg.forward(1, rows // 4)
    order = sorted(range(1, rows), key=lambda t: (-bin(t // 2).count("1"), t % 2, t))
    for t in order:
        g_copy(t).start()
    gin[0, pl.ds(0, 2)] = gout[0]

    is_end = (d == 0) | (d == last_d)
    is_next = (d == 1) | (d == last_d - 1)
    inner = jnp.where(d < 2, 1 - d, 2 * last_d - 1 - d)
    inner = jnp.where(d < 2, inner, jnp.where(d >= last_d - 1, inner, 0))
    end_id = (inner, me)
    passed = (depth - 2) * share
    kept = passed + share
    low = jnp.where(d < 2, 2 * share, 0)
    next_low = jnp.where(d < 2, share, passed)
    window = min(WINDOW, passed)

    def feat_copy(src, dst, n):
        return pltpu.make_async_remote_copy(
            src_ref=src,
            dst_ref=dst,
            send_sem=feat_ssem.at[n],
            recv_sem=feat_rsem.at[n],
            device_id=end_id,
            device_id_type=MESH,
        )

    def dy_feat():
        return feat_copy(dy_t, dy_t2, 0)

    def x_feat():
        at = pl.ds(low, passed)
        return feat_copy(xpick.at[at], x2.at[at], 1)

    def x_next_feat():
        at = pl.ds(next_low, share)
        return feat_copy(xpick.at[at], x2.at[at], 3)

    def g_feat():
        return feat_copy(g_t, g_t2, 2)

    def h_feat(s):
        return pltpu.make_async_remote_copy(
            src_ref=hpick.at[s],
            dst_ref=h2.at[s],
            send_sem=h2s_sem.at[s],
            recv_sem=h2r_sem.at[s],
            device_id=end_id,
            device_id_type=MESH,
        )

    for j in range(tiles):
        dy_t[j] = dyt[j].astype(F32).T.astype(BF16)

    @pl.when(is_end)
    def _():
        dy_feat().start()

    def g_table(t, carry):
        p = peer(me, t, bits)
        count = cnt[p]
        seen = jnp.int32(0)
        rank = [jnp.int32(2) for _ in range(tiles)]
        for s in range(slots):
            off = tcol[p, s] - me * tiles
            off = jnp.where(s < count, off, -1)
            for j in range(tiles):
                rank[j] = jnp.where(off == j, seen, rank[j])
            seen = jnp.where((off >= 0) & (off < tiles), 1, seen)
        for j in range(tiles):
            gtab[t * tiles + j] = rank[j]
        return carry

    lax.fori_loop(0, rows, g_table, 0)

    xg.forward(rows // 4, rows)

    def h_body(n, carry):
        for u in range(group):
            s = n * group + u
            x = xbuf[tcol[me, s]]
            xpick[s] = x
            terms[s] = lax.dot_general(
                x, adj[s], (((1,), (1,)), ((), ())), preferred_element_type=F32
            )
        return carry

    lax.fori_loop(0, slots // group, h_body, 0)

    @pl.when(is_end)
    def _():
        x_feat().start()

    chunk = min(32, feat)

    def h_sum(c, n, carry):
        at = pl.ds(pl.multiple_of(n * chunk, chunk), chunk)
        total = [jnp.zeros((chunk, half), F32) for _ in range(tiles)]
        for s in range(slots):
            term = terms[s, at, c * half : (c + 1) * half]
            row = jnp.where(s < my_count, trow[me, s], -1)
            for i in range(tiles):
                total[i] = total[i] + jnp.where(row == i, term, 0.0)
        for i in range(tiles):
            hbuf[c][me * tiles + i, at, :] = total[i].astype(BF16)
        return carry

    for c in range(PIECES):
        lax.fori_loop(0, feat // chunk, functools.partial(h_sum, c), 0)
        hg[c].start()
        hg[c].forward(1, rows // 4)

    for t in range(1, rows):
        g_copy(t).wait_recv()

    def g_sum(t, carry):
        for j in range(tiles):
            gacc[j] += gin[t, gtab[t * tiles + j]].astype(F32)
        return carry

    lax.fori_loop(0, rows, g_sum, 0)
    for j in range(tiles):
        g_t[j] = gacc[j].astype(BF16).astype(F32).T.astype(BF16)

    @pl.when(is_end)
    def _():
        g_feat().start()

    hg[0].forward(rows // 4, rows)

    def up_slot(n):
        return (last_d - n // share) * share + n % share

    def end_slot(n):
        return jnp.where(d == 0, up_slot(n), n)

    def h_send(c, n, carry):
        s = end_slot(n)
        hpick[c * slots + s] = hbuf[c][tcol[me, s]]

        @pl.when(n >= window)
        def _():
            h_feat(c * slots + end_slot(n - window)).wait_send()

        h_feat(c * slots + s).start()
        return carry

    def h_send_all(c):
        lax.fori_loop(0, passed, functools.partial(h_send, c), 0)
        if c == 0:
            x_next_feat().start()
        lax.fori_loop(passed, kept, functools.partial(h_send, c), 0)

    @pl.when(is_end)
    def _():
        h_send_all(0)

    @pl.when(is_next)
    def _():
        dy_feat().wait_recv()
        x_feat().wait_recv()
        g_feat().wait_recv()

    def partial(s, c, with_end=False):
        row = trow[me, s]
        col = tcol[me, s]
        cols = slice(c * half, (c + 1) * half)
        lhs = [dy_t[row], g_t[row]]
        rhs = [hbuf[c][col], xbuf[col, :, cols]]
        if with_end:
            lhs += [dy_t2[row], g_t2[row]]
            rhs += [h2[c * slots + s], x2[s, :, cols]]
        return jnp.dot(
            jnp.concatenate(lhs, axis=1),
            jnp.concatenate(rhs, axis=0),
            preferred_element_type=F32,
        )

    def up_copy(s):
        return pltpu.make_async_remote_copy(
            src_ref=send_up.at[s],
            dst_ref=recv_up.at[s],
            send_sem=us_sem.at[s],
            recv_sem=ur_sem.at[s],
            device_id=((d + 1) % depth, me),
            device_id_type=MESH,
        )

    def dn_copy(s):
        return pltpu.make_async_remote_copy(
            src_ref=send_dn.at[s],
            dst_ref=recv_dn.at[s],
            send_sem=ds_sem.at[s],
            recv_sem=dr_sem.at[s],
            device_id=((d + depth - 1) % depth, me),
            device_id_type=MESH,
        )

    def up_step(n, c):
        s = up_slot(n)
        at = c * slots + s

        @pl.when((d == 1) & (n < (last_d - 1) * share))
        def _():
            h_feat(at).wait_recv()
            send_up[at] = partial(s, c, True).astype(BF16)

            @pl.when(n >= window)
            def _():
                up_copy(c * slots + up_slot(n - window)).wait_send()

            up_copy(at).start()

        @pl.when((d > 1) & (d < last_d) & (n < (last_d - d) * share))
        def _():
            p = partial(s, c)
            up_copy(at).wait_recv()
            send_up[at] = (p + recv_up[at].astype(F32)).astype(BF16)
            up_copy(at).start()

    def dn_step(n, c):
        at = c * slots + n

        @pl.when((d == last_d - 1) & (n < d * share))
        def _():
            h_feat(at).wait_recv()
            send_dn[at] = partial(n, c, True).astype(BF16)

            @pl.when(n >= window)
            def _():
                dn_copy(at - window).wait_send()

            dn_copy(at).start()

        @pl.when((d > 0) & (d < last_d - 1) & (n < d * share))
        def _():
            p = partial(n, c)
            dn_copy(at).wait_recv()
            send_dn[at] = (p + recv_dn[at].astype(F32)).astype(BF16)
            dn_copy(at).start()

    lag = 1

    z_end = (last_d - 1) * share + lag
    is_inner = (d > 0) & (d < last_d)

    def own_step(k, c):
        s = d * share + k
        cols = slice(c * half, (c + 1) * half)

        @pl.when(is_next)
        def _():
            if c == 0:

                @pl.when(k == 0)
                def _():
                    x_next_feat().wait_recv()

            h_feat(c * slots + s).wait_recv()
            out[k, :, cols] = partial(s, c, True)

        @pl.when((d != 1) & (d != last_d - 1))
        def _():
            out[k, :, cols] = partial(s, c)

    def z_body(c, n, carry):
        @pl.when(d < last_d - 1)
        def _():
            up_step(n, c)

            @pl.when(n >= lag)
            def _():
                dn_step(n - lag, c)

        @pl.when(d == last_d - 1)
        def _():
            dn_step(n, c)

            @pl.when(n >= lag)
            def _():
                up_step(n - lag, c)

        @pl.when(n >= z_end - share)
        def _():
            own_step(n - (z_end - share), c)

        return carry

    def z_range(c, begin, end):
        @pl.when(is_inner)
        def _():
            lax.fori_loop(begin, end, functools.partial(z_body, c), 0)

    def own_range(c):
        @pl.when(is_end)
        def _():
            lax.fori_loop(0, share, lambda k, carry: (own_step(k, c), carry)[1], 0)

    for c in range(PIECES):
        z_mid = z_end // 2 if c + 1 < PIECES else z_end
        z_range(c, 0, z_mid)
        own_range(c)
        if c + 1 < PIECES:
            hg[c + 1].forward(rows // 4, rows)

            @pl.when(is_end)
            def _():
                h_send_all(c + 1)

        z_range(c, z_mid, z_end)

    def result_copy(k):
        return pltpu.make_async_copy(
            out.at[k], out_hbm.at[0, k], local_sem.at[2 * tiles + 4 + k]
        )

    def finish(k, carry):
        s = d * share + k
        for c in range(PIECES):
            at = c * slots + s
            cols = slice(c * half, (c + 1) * half)

            @pl.when(d >= 2)
            def _():
                up_copy(at).wait_recv()

            @pl.when(d <= last_d - 2)
            def _():
                dn_copy(at).wait_recv()

            total = out[k, :, cols] + recv_up[at].astype(F32) + recv_dn[at].astype(F32)
            out[k, :, cols] = jnp.where(s < my_count, total, 0.0)
        result_copy(k).start()
        return carry

    lax.fori_loop(0, share, finish, 0)

    xg.drain()
    for c in range(PIECES):
        hg[c].drain()
    for t in range(1, rows):
        g_copy(t).wait_send()

    @pl.when(is_end)
    def _():
        dy_feat().wait_send()
        x_feat().wait_send()
        g_feat().wait_send()

        x_next_feat().wait_send()
        for c in range(PIECES):
            for n in range(kept - window, kept):
                h_feat(c * slots + end_slot(n)).wait_send()

    for c in range(PIECES):
        for n in range(passed - window, passed):

            @pl.when(d == 1)
            def _():
                up_copy(c * slots + up_slot(n)).wait_send()

            @pl.when(d == last_d - 1)
            def _():
                dn_copy(c * slots + n).wait_send()

    def z_drain(s, carry):
        t = s // share

        @pl.when((d > 1) & (d < last_d) & (t > d))
        def _():
            for c in range(PIECES):
                up_copy(c * slots + s).wait_send()

        @pl.when((d > 0) & (d < last_d - 1) & (t < d))
        def _():
            for c in range(PIECES):
                dn_copy(c * slots + s).wait_send()

        return carry

    lax.fori_loop(0, slots, z_drain, 0)
    for k in range(share):
        result_copy(k).wait()


def body(rows, depth, node_feat, grad_out, adjacency, tile_count, tile_row, tile_col):
    slots, tile = adjacency.shape[:2]
    feat = node_feat.shape[0]
    tiles = node_feat.shape[1] // tile
    share = slots // depth
    dma = pltpu.SemaphoreType.DMA
    hbm = pl.BlockSpec(memory_space=pltpu.HBM)
    ntiles = rows * tiles
    turned = pltpu.VMEM((tiles, tile, feat), BF16)
    picked = pltpu.VMEM((slots, feat, tile), BF16)
    picked_half = pltpu.VMEM((PIECES * slots, feat, tile // PIECES), BF16)
    sums = pltpu.VMEM((PIECES * slots, tile, tile // PIECES), BF16)
    return pl.pallas_call(
        functools.partial(kernel, rows, depth),
        out_shape=jax.ShapeDtypeStruct((1, share, tile, tile), F32),
        in_specs=[hbm] * 6,
        out_specs=hbm,
        scratch_shapes=[
            pltpu.VMEM((share, tile, tile), F32),
            pltpu.SMEM(tile_count.shape, jnp.int32),
            pltpu.SMEM(tile_row.shape, jnp.int32),
            pltpu.SMEM(tile_col.shape, jnp.int32),
            pltpu.SMEM((rows * tiles,), jnp.int32),
            pltpu.VMEM((ntiles, feat, tile), BF16),
            [pltpu.VMEM((ntiles, feat, tile // PIECES), BF16)] * PIECES,
            pltpu.VMEM((slots, tile, tile), BF16),
            pltpu.VMEM((tiles, feat, tile), BF16),
            turned,
            turned,
            turned,
            turned,
            picked,
            picked_half,
            picked,
            picked_half,
            pltpu.VMEM((slots, feat, tile), F32),
            picked,
            pltpu.VMEM((rows, 2, feat, tile), BF16),
            pltpu.VMEM((rows, 3, feat, tile), BF16),
            pltpu.VMEM((tiles, feat, tile), F32),
            sums,
            sums,
            sums,
            sums,
            dma((2 * tiles + 4 + share,)),
            dma((2 * rows,)),
            dma((2 * rows,)),
            dma((PIECES, 2 * rows)),
            dma((PIECES, 2 * rows)),
            dma((rows,)),
            dma((rows,)),
            dma((PIECES * slots,)),
            dma((PIECES * slots,)),
            dma((PIECES * slots,)),
            dma((PIECES * slots,)),
            dma((4,)),
            dma((4,)),
            dma((PIECES * slots,)),
            dma((PIECES * slots,)),
        ],
        compiler_params=pltpu.CompilerParams(
            collective_id=0, has_side_effects=True, vmem_limit_bytes=64 * 1024 * 1024
        ),
    )(node_feat, grad_out, adjacency, tile_count, tile_row, tile_col)


def solution(mesh):
    in_specs = (P("depth", "rows"), P("depth", "rows"), P("rows", None, None), P(), P(), P())
    out_specs = P("rows", "depth", None, None)
    call = functools.partial(body, mesh.shape["rows"], mesh.shape["depth"])
    return jax.shard_map(call, mesh=mesh, in_specs=in_specs, out_specs=out_specs, check_vma=False)
```

```python
import functools

import jax
import jax.numpy as jnp
from jax import lax
from jax.experimental import pallas as pl
from jax.experimental.pallas import tpu as pltpu
from jax.sharding import PartitionSpec as P

PIECES = 1
WINDOW = 2

MESH = pl.DeviceIdType.MESH
F32 = jnp.float32
BF16 = jnp.bfloat16


def flip(index, mask):
    bit = 1
    out = index
    while bit <= mask:
        if mask & bit:
            out = out + bit * (1 - 2 * ((index // bit) % 2))
        bit *= 2
    return out


def bit_orders(rows):
    bits = []
    bit = 1
    while bit < rows:
        bits.append(bit)
        bit *= 2
    core, chip = bits[:1], bits[1:]
    half = len(chip) // 2
    x_bits, y_bits = chip[:half], chip[half:]
    return (y_bits + x_bits + core, x_bits + y_bits + core)


def peer(index, mask, bits):
    out = index
    for bit in bits:
        out = out + bit * (1 - 2 * ((index // bit) % 2)) * ((mask // bit) % 2)
    return out


class Gather:
    def __init__(self, rows, tiles, buf, send_sem, recv_sem, depth_id, me):
        self.rows, self.tiles, self.buf = rows, tiles, buf
        self.send_sem, self.recv_sem = send_sem, recv_sem
        self.depth_id, self.me = depth_id, me
        self.orders = bit_orders(rows)

    def mask(self, half, place):
        out = 0
        for n, bit in enumerate(self.orders[half]):
            if place >> n & 1:
                out |= bit
        return out

    def copy(self, half, place, n):
        mask = self.mask(half, place)
        bit = self.orders[half][n]
        part = self.tiles // 2
        block = flip(self.me, mask)
        ref = self.buf.at[pl.ds(block * self.tiles + half * part, part)]
        sem = half * self.rows + (mask | bit)
        return pltpu.make_async_remote_copy(
            src_ref=ref,
            dst_ref=ref,
            send_sem=self.send_sem.at[sem],
            recv_sem=self.recv_sem.at[sem],
            device_id=(self.depth_id, flip(self.me, bit)),
            device_id_type=MESH,
        )

    def incoming(self, half, place):
        mask = self.mask(half, place)
        part = self.tiles // 2
        ref = self.buf.at[pl.ds(flip(self.me, mask) * self.tiles + half * part, part)]
        sem = half * self.rows + mask
        return pltpu.make_async_remote_copy(
            src_ref=ref,
            dst_ref=ref,
            send_sem=self.send_sem.at[sem],
            recv_sem=self.recv_sem.at[sem],
            device_id=(self.depth_id, flip(self.me, mask)),
            device_id_type=MESH,
        )

    def start(self):
        for n in range(len(self.orders[0])):
            for half in range(2):
                self.copy(half, 0, n).start()

    def forward(self, begin, end):
        count = len(self.orders[0])
        for place in range(begin, end):
            for half in range(2):
                self.incoming(half, place).wait_recv()
                for n in range(place.bit_length(), count):
                    self.copy(half, place, n).start()

    def drain(self):
        count = len(self.orders[0])
        for place in range(self.rows // 2):
            for half in range(2):
                for n in range(place.bit_length(), count):
                    self.copy(half, place, n).wait_send()


def kernel(
    rows,
    depth,
    x_hbm,
    dy_hbm,
    adj_hbm,
    cnt_hbm,
    trow_hbm,
    tcol_hbm,
    out_hbm,
    out,
    cnt,
    trow,
    tcol,
    gtab,
    xbuf,
    hbuf,
    adj,
    dyt,
    dy_t,
    g_t,
    dy_t2,
    g_t2,
    xpick,
    hpick,
    x2,
    h2,
    terms,
    gterm,
    gout,
    gin,
    gacc,
    send_up,
    send_dn,
    recv_up,
    recv_dn,
    local_sem,
    xs_sem,
    xr_sem,
    hs_sem,
    hr_sem,
    gs_sem,
    gr_sem,
    us_sem,
    ur_sem,
    ds_sem,
    dr_sem,
    feat_ssem,
    feat_rsem,
    h2s_sem,
    h2r_sem,
):
    d = lax.axis_index("depth")
    me = lax.axis_index("rows")
    feat = xbuf.shape[1]
    tile = xbuf.shape[2]
    tiles = dyt.shape[0]
    slots = adj.shape[0]
    share = slots // depth
    last_d = depth - 1
    group = 4
    bits = sorted(bit_orders(rows)[0])

    x_local, dy_local = [], []
    for j in range(tiles):
        cols = pl.ds(j * tile, tile)
        x_local.append(
            pltpu.make_async_copy(x_hbm.at[:, cols], xbuf.at[me * tiles + j], local_sem.at[j])
        )
        dy_local.append(
            pltpu.make_async_copy(dy_hbm.at[:, cols], dyt.at[j], local_sem.at[tiles + j])
        )
    adj_local = pltpu.make_async_copy(adj_hbm, adj, local_sem.at[2 * tiles])
    table_local = [
        pltpu.make_async_copy(src, dst, local_sem.at[2 * tiles + 1 + n])
        for n, (src, dst) in enumerate(((cnt_hbm, cnt), (trow_hbm, trow), (tcol_hbm, tcol)))
    ]
    for c in x_local + table_local + dy_local + [adj_local]:
        c.start()

    barrier = pltpu.get_barrier_semaphore()
    for t in range(1, rows):
        pl.semaphore_signal(
            barrier, inc=1, device_id=(d, (me + t) % rows), device_id_type=MESH
        )
    for t in range(1, depth):
        pl.semaphore_signal(
            barrier, inc=1, device_id=((d + t) % depth, me), device_id_type=MESH
        )

    for c in range(PIECES):
        at = pl.ds(c * slots + d * share, share)

        @pl.when(d <= 1)
        def _():
            recv_up[at] = jnp.zeros((share,) + recv_up.shape[1:], BF16)

        @pl.when(d >= last_d - 1)
        def _():
            recv_dn[at] = jnp.zeros((share,) + recv_dn.shape[1:], BF16)

    for t in range(rows):
        gin[t, 2] = jnp.zeros((feat, tile), BF16)
    gacc[...] = jnp.zeros_like(gacc)

    pl.semaphore_wait(barrier, rows - 1 + depth - 1)

    for c in x_local:
        c.wait()
    xg = Gather(rows, tiles, xbuf, xs_sem, xr_sem, d, me)
    hg = [
        Gather(rows, tiles, hbuf[c], hs_sem.at[c], hr_sem.at[c], d, me) for c in range(PIECES)
    ]
    half = tile // PIECES
    xg.start()
    for c in table_local + dy_local + [adj_local]:
        c.wait()

    my_count = cnt[me]

    def g_body(n, carry):
        for u in range(group):
            s = n * group + u
            g = jnp.dot(dyt[trow[me, s]], adj[s], preferred_element_type=F32)
            gterm[s] = g.astype(BF16)
        return carry

    lax.fori_loop(0, slots // group, g_body, 0)

    def g_pick(t, carry):
        o = peer(me, t, bits)
        first = jnp.int32(0)
        last = jnp.int32(0)
        seen = jnp.int32(0)
        for s in range(slots):
            hit = (s < my_count) & (lax.div(tcol[me, s], jnp.int32(tiles)) == o)
            last = jnp.where(hit, s, last)
            first = jnp.where(hit & (seen == 0), s, first)
            seen = jnp.where(hit, 1, seen)
        gout[t, 0] = gterm[first]
        gout[t, 1] = gterm[last]
        return carry

    lax.fori_loop(0, rows, g_pick, 0)

    def g_copy(t):
        return pltpu.make_async_remote_copy(
            src_ref=gout.at[t],
            dst_ref=gin.at[t, pl.ds(0, 2)],
            send_sem=gs_sem.at[t],
            recv_sem=gr_sem.at[t],
            device_id=(d, flip(me, t)),
            device_id_type=MESH,
        )

    xg.forward(1, rows // 2)
    order = sorted(range(1, rows), key=lambda t: (-bin(t // 2).count("1"), t % 2, t))
    for t in order:
        g_copy(t).start()
    gin[0, pl.ds(0, 2)] = gout[0]

    is_end = (d == 0) | (d == last_d)
    is_next = (d == 1) | (d == last_d - 1)
    inner = jnp.where(d < 2, 1 - d, 2 * last_d - 1 - d)
    inner = jnp.where(d < 2, inner, jnp.where(d >= last_d - 1, inner, 0))
    end_id = (inner, me)
    passed = (depth - 2) * share
    kept = passed + share
    low = jnp.where(d < 2, 2 * share, 0)
    next_low = jnp.where(d < 2, share, passed)
    window = min(WINDOW, passed)

    def feat_copy(src, dst, n):
        return pltpu.make_async_remote_copy(
            src_ref=src,
            dst_ref=dst,
            send_sem=feat_ssem.at[n],
            recv_sem=feat_rsem.at[n],
            device_id=end_id,
            device_id_type=MESH,
        )

    def dy_feat():
        return feat_copy(dy_t, dy_t2, 0)

    def x_feat():
        at = pl.ds(low, passed)
        return feat_copy(xpick.at[at], x2.at[at], 1)

    def x_next_feat():
        at = pl.ds(next_low, share)
        return feat_copy(xpick.at[at], x2.at[at], 3)

    def g_feat():
        return feat_copy(g_t, g_t2, 2)

    def h_feat(s):
        return pltpu.make_async_remote_copy(
            src_ref=hpick.at[s],
            dst_ref=h2.at[s],
            send_sem=h2s_sem.at[s],
            recv_sem=h2r_sem.at[s],
            device_id=end_id,
            device_id_type=MESH,
        )

    for j in range(tiles):
        dy_t[j] = dyt[j].astype(F32).T.astype(BF16)

    @pl.when(is_end)
    def _():
        dy_feat().start()

    def g_table(t, carry):
        p = peer(me, t, bits)
        count = cnt[p]
        seen = jnp.int32(0)
        rank = [jnp.int32(2) for _ in range(tiles)]
        for s in range(slots):
            off = tcol[p, s] - me * tiles
            off = jnp.where(s < count, off, -1)
            for j in range(tiles):
                rank[j] = jnp.where(off == j, seen, rank[j])
            seen = jnp.where((off >= 0) & (off < tiles), 1, seen)
        for j in range(tiles):
            gtab[t * tiles + j] = rank[j]
        return carry

    lax.fori_loop(0, rows, g_table, 0)

    xg.forward(rows // 2, rows)

    def h_body(n, carry):
        for u in range(group):
            s = n * group + u
            x = xbuf[tcol[me, s]]
            xpick[s] = x
            terms[s] = lax.dot_general(
                x, adj[s], (((1,), (1,)), ((), ())), preferred_element_type=F32
            )
        return carry

    lax.fori_loop(0, slots // group, h_body, 0)

    @pl.when(is_end)
    def _():
        x_feat().start()

    chunk = min(32, feat)

    def h_sum(c, n, carry):
        at = pl.ds(pl.multiple_of(n * chunk, chunk), chunk)
        total = [jnp.zeros((chunk, half), F32) for _ in range(tiles)]
        for s in range(slots):
            term = terms[s, at, c * half : (c + 1) * half]
            row = jnp.where(s < my_count, trow[me, s], -1)
            for i in range(tiles):
                total[i] = total[i] + jnp.where(row == i, term, 0.0)
        for i in range(tiles):
            hbuf[c][me * tiles + i, at, :] = total[i].astype(BF16)
        return carry

    for c in range(PIECES):
        lax.fori_loop(0, feat // chunk, functools.partial(h_sum, c), 0)
        hg[c].start()
        hg[c].forward(1, rows // 4)

    for t in range(1, rows):
        g_copy(t).wait_recv()

    def g_sum(t, carry):
        for j in range(tiles):
            gacc[j] += gin[t, gtab[t * tiles + j]].astype(F32)
        return carry

    lax.fori_loop(0, rows, g_sum, 0)
    for j in range(tiles):
        g_t[j] = gacc[j].astype(BF16).astype(F32).T.astype(BF16)

    @pl.when(is_end)
    def _():
        g_feat().start()

    hg[0].forward(rows // 4, rows)

    def up_slot(n):
        return (last_d - n // share) * share + n % share

    def end_slot(n):
        return jnp.where(d == 0, up_slot(n), n)

    def h_send(c, n, carry):
        s = end_slot(n)
        hpick[c * slots + s] = hbuf[c][tcol[me, s]]

        @pl.when(n >= window)
        def _():
            h_feat(c * slots + end_slot(n - window)).wait_send()

        h_feat(c * slots + s).start()
        return carry

    def h_send_all(c):
        lax.fori_loop(0, passed, functools.partial(h_send, c), 0)
        if c == 0:
            x_next_feat().start()
        lax.fori_loop(passed, kept, functools.partial(h_send, c), 0)

    @pl.when(is_end)
    def _():
        h_send_all(0)

    @pl.when(is_next)
    def _():
        dy_feat().wait_recv()
        x_feat().wait_recv()
        g_feat().wait_recv()

    def partial(s, c, with_end=False):
        row = trow[me, s]
        col = tcol[me, s]
        cols = slice(c * half, (c + 1) * half)
        lhs = [dy_t[row], g_t[row]]
        rhs = [hbuf[c][col], xbuf[col, :, cols]]
        if with_end:
            lhs += [dy_t2[row], g_t2[row]]
            rhs += [h2[c * slots + s], x2[s, :, cols]]
        return jnp.dot(
            jnp.concatenate(lhs, axis=1),
            jnp.concatenate(rhs, axis=0),
            preferred_element_type=F32,
        )

    def up_copy(s):
        return pltpu.make_async_remote_copy(
            src_ref=send_up.at[s],
            dst_ref=recv_up.at[s],
            send_sem=us_sem.at[s],
            recv_sem=ur_sem.at[s],
            device_id=((d + 1) % depth, me),
            device_id_type=MESH,
        )

    def dn_copy(s):
        return pltpu.make_async_remote_copy(
            src_ref=send_dn.at[s],
            dst_ref=recv_dn.at[s],
            send_sem=ds_sem.at[s],
            recv_sem=dr_sem.at[s],
            device_id=((d + depth - 1) % depth, me),
            device_id_type=MESH,
        )

    def up_step(n, c):
        s = up_slot(n)
        at = c * slots + s

        @pl.when((d == 1) & (n < (last_d - 1) * share))
        def _():
            h_feat(at).wait_recv()
            send_up[at] = partial(s, c, True).astype(BF16)

            @pl.when(n >= window)
            def _():
                up_copy(c * slots + up_slot(n - window)).wait_send()

            up_copy(at).start()

        @pl.when((d > 1) & (d < last_d) & (n < (last_d - d) * share))
        def _():
            p = partial(s, c)
            up_copy(at).wait_recv()
            send_up[at] = (p + recv_up[at].astype(F32)).astype(BF16)
            up_copy(at).start()

    def dn_step(n, c):
        at = c * slots + n

        @pl.when((d == last_d - 1) & (n < d * share))
        def _():
            h_feat(at).wait_recv()
            send_dn[at] = partial(n, c, True).astype(BF16)

            @pl.when(n >= window)
            def _():
                dn_copy(at - window).wait_send()

            dn_copy(at).start()

        @pl.when((d > 0) & (d < last_d - 1) & (n < d * share))
        def _():
            p = partial(n, c)
            dn_copy(at).wait_recv()
            send_dn[at] = (p + recv_dn[at].astype(F32)).astype(BF16)
            dn_copy(at).start()

    lag = 1

    z_end = (last_d - 1) * share + lag
    is_inner = (d > 0) & (d < last_d)

    def own_step(k, c):
        s = d * share + k
        cols = slice(c * half, (c + 1) * half)

        @pl.when(is_next)
        def _():
            if c == 0:

                @pl.when(k == 0)
                def _():
                    x_next_feat().wait_recv()

            h_feat(c * slots + s).wait_recv()
            out[k, :, cols] = partial(s, c, True)

        @pl.when((d != 1) & (d != last_d - 1))
        def _():
            out[k, :, cols] = partial(s, c)

    def z_body(c, n, carry):
        @pl.when(d < last_d - 1)
        def _():
            up_step(n, c)

            @pl.when(n >= lag)
            def _():
                dn_step(n - lag, c)

        @pl.when(d == last_d - 1)
        def _():
            dn_step(n, c)

            @pl.when(n >= lag)
            def _():
                up_step(n - lag, c)

        @pl.when(n >= z_end - share)
        def _():
            own_step(n - (z_end - share), c)

        return carry

    def z_range(c, begin, end):
        @pl.when(is_inner)
        def _():
            lax.fori_loop(begin, end, functools.partial(z_body, c), 0)

    def own_range(c):
        @pl.when(is_end)
        def _():
            lax.fori_loop(0, share, lambda k, carry: (own_step(k, c), carry)[1], 0)

    for c in range(PIECES):
        z_mid = z_end // 2 if c + 1 < PIECES else z_end
        z_range(c, 0, z_mid)
        own_range(c)
        if c + 1 < PIECES:
            hg[c + 1].forward(rows // 4, rows)

            @pl.when(is_end)
            def _():
                h_send_all(c + 1)

        z_range(c, z_mid, z_end)

    def result_copy(k):
        return pltpu.make_async_copy(
            out.at[k], out_hbm.at[0, k], local_sem.at[2 * tiles + 4 + k]
        )

    def finish(k, carry):
        s = d * share + k
        for c in range(PIECES):
            at = c * slots + s
            cols = slice(c * half, (c + 1) * half)

            @pl.when(d >= 2)
            def _():
                up_copy(at).wait_recv()

            @pl.when(d <= last_d - 2)
            def _():
                dn_copy(at).wait_recv()

            total = out[k, :, cols] + recv_up[at].astype(F32) + recv_dn[at].astype(F32)
            out[k, :, cols] = jnp.where(s < my_count, total, 0.0)
        result_copy(k).start()
        return carry

    lax.fori_loop(0, share, finish, 0)

    xg.drain()
    for c in range(PIECES):
        hg[c].drain()
    for t in range(1, rows):
        g_copy(t).wait_send()

    @pl.when(is_end)
    def _():
        dy_feat().wait_send()
        x_feat().wait_send()
        g_feat().wait_send()

        x_next_feat().wait_send()
        for c in range(PIECES):
            for n in range(kept - window, kept):
                h_feat(c * slots + end_slot(n)).wait_send()

    for c in range(PIECES):
        for n in range(passed - window, passed):

            @pl.when(d == 1)
            def _():
                up_copy(c * slots + up_slot(n)).wait_send()

            @pl.when(d == last_d - 1)
            def _():
                dn_copy(c * slots + n).wait_send()

    def z_drain(s, carry):
        t = s // share

        @pl.when((d > 1) & (d < last_d) & (t > d))
        def _():
            for c in range(PIECES):
                up_copy(c * slots + s).wait_send()

        @pl.when((d > 0) & (d < last_d - 1) & (t < d))
        def _():
            for c in range(PIECES):
                dn_copy(c * slots + s).wait_send()

        return carry

    lax.fori_loop(0, slots, z_drain, 0)
    for k in range(share):
        result_copy(k).wait()


def body(rows, depth, node_feat, grad_out, adjacency, tile_count, tile_row, tile_col):
    slots, tile = adjacency.shape[:2]
    feat = node_feat.shape[0]
    tiles = node_feat.shape[1] // tile
    share = slots // depth
    dma = pltpu.SemaphoreType.DMA
    hbm = pl.BlockSpec(memory_space=pltpu.HBM)
    ntiles = rows * tiles
    turned = pltpu.VMEM((tiles, tile, feat), BF16)
    picked = pltpu.VMEM((slots, feat, tile), BF16)
    picked_half = pltpu.VMEM((PIECES * slots, feat, tile // PIECES), BF16)
    sums = pltpu.VMEM((PIECES * slots, tile, tile // PIECES), BF16)
    return pl.pallas_call(
        functools.partial(kernel, rows, depth),
        out_shape=jax.ShapeDtypeStruct((1, share, tile, tile), F32),
        in_specs=[hbm] * 6,
        out_specs=hbm,
        scratch_shapes=[
            pltpu.VMEM((share, tile, tile), F32),
            pltpu.SMEM(tile_count.shape, jnp.int32),
            pltpu.SMEM(tile_row.shape, jnp.int32),
            pltpu.SMEM(tile_col.shape, jnp.int32),
            pltpu.SMEM((rows * tiles,), jnp.int32),
            pltpu.VMEM((ntiles, feat, tile), BF16),
            [pltpu.VMEM((ntiles, feat, tile // PIECES), BF16)] * PIECES,
            pltpu.VMEM((slots, tile, tile), BF16),
            pltpu.VMEM((tiles, feat, tile), BF16),
            turned,
            turned,
            turned,
            turned,
            picked,
            picked_half,
            picked,
            picked_half,
            pltpu.VMEM((slots, feat, tile), F32),
            picked,
            pltpu.VMEM((rows, 2, feat, tile), BF16),
            pltpu.VMEM((rows, 3, feat, tile), BF16),
            pltpu.VMEM((tiles, feat, tile), F32),
            sums,
            sums,
            sums,
            sums,
            dma((2 * tiles + 4 + share,)),
            dma((2 * rows,)),
            dma((2 * rows,)),
            dma((PIECES, 2 * rows)),
            dma((PIECES, 2 * rows)),
            dma((rows,)),
            dma((rows,)),
            dma((PIECES * slots,)),
            dma((PIECES * slots,)),
            dma((PIECES * slots,)),
            dma((PIECES * slots,)),
            dma((4,)),
            dma((4,)),
            dma((PIECES * slots,)),
            dma((PIECES * slots,)),
        ],
        compiler_params=pltpu.CompilerParams(
            collective_id=0, has_side_effects=True, vmem_limit_bytes=64 * 1024 * 1024
        ),
    )(node_feat, grad_out, adjacency, tile_count, tile_row, tile_col)


def solution(mesh):
    in_specs = (P("depth", "rows"), P("depth", "rows"), P("rows", None, None), P(), P(), P())
    out_specs = P("rows", "depth", None, None)
    call = functools.partial(body, mesh.shape["rows"], mesh.shape["depth"])
    return jax.shard_map(call, mesh=mesh, in_specs=in_specs, out_specs=out_specs, check_vma=False)
```
